512 devices in a mesh: mem: 4 (over x), gx: 16 (over z_lo, core), gy: 8 (over y, z_hi).
Axes of the slice: x: 4, y: 4, z: 16 (z_hi: 2, z_lo: 8; z = z_hi * 8 + z_lo), core: 2. Of those that a mesh axis runs over, the one named last changes fastest.
Arguments:
- members: bfloat16 [8, 64, 256, 1024], P('mem', None, 'gx', 'gy'), may hold values from -6 to 6
- gradient: float32 [64, 256, 1024], P(None, 'gx', 'gy'), may hold values from -6 to 6
- control: bfloat16 [8, 64, 256, 1024], P('mem', None, 'gx', 'gy'), may hold values from -6 to 6
- filter_rates: float32 [64], replicated, may hold values from 0.0009765625 to 0.03
- vertical_weights: float32 [64, 64], replicated, may hold values from -0.75 to 0.75
- band_widths: int32 [64], replicated, may hold values from 0 to 63, each once
Outputs:
- control_gradient: float32 [8, 64, 256, 1024], P('mem', None, 'gx', 'gy')
The draws below stay inside these ranges and needn't reach their ends.
Inputs may be any that keep to these rules, and one draw needn't show every extreme that they name: `band_widths`: each of the values 0 to 63 appears once.
All inputs are finite; a program needn't handle non-finite values.
Results may differ from the reference program's by a relative error of at most 0.0003.
Values sent between devices are 32-bit elements; how exact they have to be, the bound alone decides.
A program may use at most 64 MiB of HBM per device.

```python
import math
import jax
import jax.numpy as jnp
from jax import lax

LEV = 64
NPASS = 2
MEMBERS = 8
NX = 256
NY = 1024


def steps_of(stream_key, shape, split, smallest, high):
    def one(axis_at, blocks):
        heights = jax.random.uniform(jax.random.fold_in(jax.random.fold_in(stream_key, 6), axis_at), (blocks,), jnp.float32, smallest / len(split), high / len(split))
        return jnp.repeat(jnp.exp(heights), shape[axis_at] // blocks).reshape((-1,) + (1,) * (len(shape) - axis_at - 1))

    level = one(*split[0])
    for cut in split[1:]:
        level = level * one(*cut)
    return level


def centred(own_key, shape, scale, limit, cuts=(), kind=jnp.bfloat16):
    result = jax.random.normal(own_key, shape, jnp.float32) * scale
    if len(cuts) > 0:
        result = steps_of(own_key, shape, cuts, -0.22, 0.18) * result
    return jnp.clip(result, min=-limit, max=limit).astype(kind)


def setup_inputs(seed: int = 0) -> dict:
    key_of = jax.random.split(jax.random.key(seed), 7)
    members = centred(key_of[0], (MEMBERS, LEV, NX, NY), 1.0, 6.0, ((0, 4), (2, 16), (3, 8)))
    gradient = centred(key_of[1], (LEV, NX, NY), 1.0, 6.0, ((1, 16), (2, 8)), jnp.float32)
    control = centred(key_of[2], (MEMBERS, LEV, NX, NY), 1.0, 6.0, ((0, 4), (2, 16), (3, 8)))
    filter_rates = jnp.clip(jnp.exp(jax.random.uniform(key_of[3], (LEV,), jnp.float32, math.log(0.0009765625), math.log(0.03))), 0.0009765625, 0.03)
    vertical_weights = centred(key_of[4], (LEV, LEV), LEV ** -0.5, 0.75, (), jnp.float32)
    band_widths = jax.random.permutation(key_of[5], LEV).astype(jnp.int32)
    return dict(members=members, gradient=gradient, control=control, filter_rates=filter_rates, vertical_weights=vertical_weights, band_widths=band_widths)


highest = lax.Precision.HIGHEST


def sweep_lines(field, decays, axis, backward):
    moved = jnp.moveaxis(field, axis, 0)
    shaped = decays[:, None]

    def advance(running, cell):
        running = shaped * running + (1.0 - shaped) * cell
        return running, running

    _, swept = lax.scan(advance, jnp.zeros_like(moved[0]), moved, reverse=backward)
    return jnp.moveaxis(swept, 0, axis)


def reference(members, gradient, control, filter_rates, vertical_weights, band_widths):
    def accumulate(running, member):
        return running + member.astype(jnp.float32), None

    summed, _ = lax.scan(accumulate, jnp.zeros(members.shape[1:], jnp.float32), members)
    ensemble_mean = summed / MEMBERS
    decays = 1.0 - filter_rates
    level_ids = jnp.arange(LEV)
    keep = jnp.abs(level_ids[:, None] - level_ids[None, :]) <= band_widths[None, :]
    masked = jnp.where(keep, vertical_weights, jnp.zeros_like(vertical_weights))

    def one_member(paired):
        member, own_control = paired
        field = (member.astype(jnp.float32) - ensemble_mean) * gradient
        for repeat in range(NPASS):
            field = sweep_lines(field, decays, 1, False)
            field = sweep_lines(field, decays, 1, True)
        for repeat in range(NPASS):
            field = sweep_lines(field, decays, 2, False)
            field = sweep_lines(field, decays, 2, True)
        field = field * (2.0 / filter_rates)[:, None, None]
        mixed = jnp.einsum("pl,pxy->lxy", masked, field, precision=highest)
        return mixed + own_control.astype(jnp.float32)

    return lax.map(one_member, (members, control))
```

```python
import functools

import jax
import jax.numpy as jnp
from jax import lax
from jax.experimental import pallas as pl
from jax.experimental.pallas import tpu as pltpu
from jax.sharding import PartitionSpec as P

MESH = pl.DeviceIdType.MESH
F32 = jnp.float32
BF16 = jnp.bfloat16

LEV, MEMBERS, NX, NY = 64, 8, 256, 1024
MEM, GX, GY = 4, 16, 8
KLOC = MEMBERS // MEM
BX, BY = NX // GX, NY // GY
ROWS = LEV * BX
GROUPS = LEV // 4
QUARTER = ROWS // MEM
CHUNKS = 4
CHUNK = LEV // CHUNKS

NT = (((1,), (1,)), ((), ()))
NN = (((1,), (0,)), ((), ()))
TN = (((0,), (0,)), ((), ()))


def dot(a, b, dims):
    return lax.dot_general(a, b, dims, preferred_element_type=F32)


def split(x):
    hi = x.astype(BF16)
    return hi, (x - hi.astype(F32)).astype(BF16)


def iota(shape, axis):
    return lax.broadcasted_iota(jnp.int32, shape, axis)


class Line:
    def __init__(self, rate, total, size, index):
        r = rate
        self.rate = r
        self.log = -r * (1.0 + r * (0.5 + r * (1.0 / 3 + r * (0.25 + r * (0.2 + r * (1.0 / 6))))))
        self.a = 1.0 - r
        self.g = self.a * self.a / (r * (1.0 + self.a))
        self.s = (index * size).astype(F32)
        self.last = self.s + (size - 1.0)
        self.n2 = 2.0 * total - self.last
        self.p_s = self.power(self.s)
        self.p_inv = self.power(-self.last)
        self.p_n2 = self.power(self.n2)
        self.ga = self.g * self.power(2.0 * total)
        self.G = 1.0 + 2.0 * self.g + self.ga
        self.total = total
        self.e = self.s + size

    def power(self, m):
        return jnp.exp(self.log * m)

    def sums(self, r1, r2, q1, q2):
        sa = self.p_inv * r1
        fq = self.p_s * q1
        sb = self.p_inv * (self.last * r1 - r2) + self.g * fq
        lh = fq - self.p_n2 * r1
        la = self.p_s * ((self.s + self.G) * q1 + q2) - self.p_n2 * ((self.n2 + self.G) * r1 + r2)
        return sa, sb, la, lh


def kernel(rates, rates_v, bands, weights, members, gradient, control, out,
           mem_v, grad_v, ctl_v, out_v, psum, total, rs_rcv, vbuf, zbuf, wtab, lsub, thi, tlo,
           mu, ysnd, yrcv, zsnd, zrcv, kap, xst, xpair, xin, xout, xss, xsr, fbuf,
           in_sem, rs_s, rs_r, ag_s, ag_r, y_s, y_r, h_s, h_r, p_s, p_r, c_s, c_r, d_s, d_r):
    i = lax.axis_index("mem")
    gx = lax.axis_index("gx")
    gy = lax.axis_index("gy")
    z, core = gx // 2, gx % 2
    yy, hh = gy // 2, gy % 2

    loads = [
        pltpu.make_async_copy(members, mem_v, in_sem.at[0]),
        pltpu.make_async_copy(gradient, grad_v, in_sem.at[1]),
        pltpu.make_async_copy(control, ctl_v, in_sem.at[2]),
    ]
    for load in loads:
        load.start()

    def signal(dev):
        pl.semaphore_signal(barrier, inc=1, device_id=dev, device_id_type=MESH)

    barrier = pltpu.get_barrier_semaphore()
    sibling = (i, gx + 1 - 2 * core, gy)
    across = (i, gx, gy + 1 - 2 * hh)
    peers = [((i + d) % MEM, gx, gy) for d in range(1, MEM)]
    y_at = [(yy + d) % 4 for d in range(1, 4)]
    signal(across)
    for d in range(3):
        signal(peers[d])
        signal((i, gx, y_at[d] * 2 + hh))
    signal(sibling)

    @pl.when(z > 0)
    def _():
        signal((i, gx - 2, gy))

    @pl.when(z < 7)
    def _():
        signal((i, gx + 2, gy))

    sub8 = iota((8, 128), 0)
    for t in range(LEV // 8):
        v = jnp.zeros((8, 128), F32)
        for j in range(8):
            v = jnp.where(sub8 == j, rates[t * 8 + j], v)
        lsub[t * 8:(t + 1) * 8, :] = v
    lane_lv = (iota((GROUPS, 128), 1) // BX) % 4
    row_g = iota((GROUPS, 128), 0)
    lev_id = row_g * 4 + lane_lv
    rate_lane = jnp.zeros((GROUPS, 128), F32)
    for l in range(LEV):
        rate_lane = jnp.where(lev_id == l, rates[l], rate_lane)
    ly = Line(rate_lane, NY, BY, gy)
    lx_rate = lsub[...]

    cell = iota((8, 128), 1).astype(F32)
    dist = jnp.where(sub8 < 2, 127.0 - cell, cell)
    factor = jnp.where((sub8 == 0) | (sub8 == 2), 1.0, jnp.where((sub8 == 1) | (sub8 == 3), dist, 0.0))

    def logs(r):
        return -r * (1.0 + r * (0.5 + r * (1.0 / 3 + r * (0.25 + r * (0.2 + r * (1.0 / 6))))))

    def basis(l, carry):
        lg = logs(jnp.broadcast_to(lsub[pl.ds(l, 1), :], (8, 128)))
        wtab[pl.ds(pl.multiple_of(l * 8, 8), 8), :] = jnp.exp(dist * lg) * factor
        return carry

    lax.fori_loop(0, LEV, basis, 0, unroll=4)

    loads[0].wait()
    for q in range(MEM):
        lo = q * QUARTER
        psum[lo:lo + QUARTER, :] = (mem_v[0, lo:lo + QUARTER, :].astype(F32)
                                    + mem_v[1, lo:lo + QUARTER, :].astype(F32))

    pl.semaphore_wait(barrier, 8 + (z > 0).astype(jnp.int32) + (z < 7).astype(jnp.int32))

    rs = []
    for d in range(3):
        at = pl.multiple_of(peers[d][0] * QUARTER, QUARTER)
        cp = pltpu.make_async_remote_copy(
            src_ref=psum.at[pl.ds(at, QUARTER)], dst_ref=rs_rcv.at[d],
            send_sem=rs_s.at[d], recv_sem=rs_r.at[d], device_id=peers[d], device_id_type=MESH)
        cp.start()
        rs.append(cp)

    di = jnp.abs(iota((BY, BY), 0) - iota((BY, BY), 1)).astype(F32)

    def toeplitz(l, carry):
        r = jnp.broadcast_to(lsub[pl.ds(l, 1), :], (8, 128))
        lg = logs(r)
        a = 1.0 - r
        c = 1.0 + 2.0 * (a * a / (r * (1.0 + a)))
        lg = jnp.broadcast_to(lg[0:1, :], (BY, BY))
        c = jnp.broadcast_to(c[0:1, :], (BY, BY))
        t = jnp.exp(di * lg) * (di + c)
        hi, lo = split(t)
        at = pl.multiple_of(l * BY, BY)
        thi[pl.ds(at, BY), :] = hi
        tlo[pl.ds(at, BY), :] = lo
        return carry

    lax.fori_loop(0, LEV, toeplitz, 0)

    own = pl.multiple_of(i * QUARTER, QUARTER)
    for cp in rs:
        cp.wait()
    total[pl.ds(own, QUARTER), :] = (psum[pl.ds(own, QUARTER), :] + rs_rcv[0] + rs_rcv[1] + rs_rcv[2])
    ag = []
    for d in range(3):
        cp = pltpu.make_async_remote_copy(
            src_ref=total.at[pl.ds(own, QUARTER)], dst_ref=total.at[pl.ds(own, QUARTER)],
            send_sem=ag_s.at[d], recv_sem=ag_r.at[d], device_id=peers[d], device_id_type=MESH)
        cp.start()
        ag.append(cp)
    loads[1].wait()
    for cp in ag:
        cp.wait()

    def product(g, carry):
        at = pl.multiple_of(g * 64, 64)
        mean = total[pl.ds(at, 64), :] * (1.0 / MEMBERS)
        gr = grad_v[pl.ds(at, 64), :]
        v0 = (mem_v[0, pl.ds(at, 64), :].astype(F32) - mean) * gr
        v1 = (mem_v[1, pl.ds(at, 64), :].astype(F32) - mean) * gr
        vbuf[0, pl.ds(at, 64), :] = v0
        vbuf[1, pl.ds(at, 64), :] = v1
        vh, vl = split(jnp.concatenate([v0, v1], axis=0))
        wh, wl = split(wtab[pl.ds(pl.multiple_of(g * 32, 32), 32), :])
        res = dot(wh, vh, NT) + dot(wh, vl, NT) + dot(wl, vh, NT)
        lane = (iota((8, 128), 1) // BX) % 4
        m8 = jnp.zeros((8, 128), F32)
        for lv in range(4):
            m8 = jnp.where(lane == lv, res[lv * 8:lv * 8 + 8, :], m8)
        mu[pl.ds(pl.multiple_of(g * 8, 8), 8), :] = m8
        return carry

    lax.fori_loop(0, GROUPS, product, 0)

    r1, r2, q1, q2 = [mu[pl.ds(q, GROUPS, stride=8), :] for q in range(4)]
    own_y = ly.sums(r1, r2, q1, q2)
    for q in range(4):
        ysnd[q] = own_y[q]
    ycp = []
    for d in range(3):
        part = pl.multiple_of(jnp.where(y_at[d] > yy, 0, 2), 2)
        cp = pltpu.make_async_remote_copy(
            src_ref=ysnd.at[pl.ds(part, 2)], dst_ref=yrcv.at[d],
            send_sem=y_s.at[d], recv_sem=y_r.at[d], device_id=(i, gx, y_at[d] * 2 + hh), device_id_type=MESH)
        cp.start()
        ycp.append(cp)

    def local_y(l, carry):
        at = pl.multiple_of(l * BX, BX)
        tt = pl.multiple_of(l * BY, BY)
        v = jnp.concatenate([vbuf[0, pl.ds(at, BX), :], vbuf[1, pl.ds(at, BX), :]], axis=0)
        vh, vl = split(v)
        th = thi[pl.ds(tt, BY), :]
        res = dot(vh, th, NN) + dot(vl, th, NN) + dot(vh, tlo[pl.ds(tt, BY), :], NN)
        zbuf[0, pl.ds(at, BX), :] = res[0:BX]
        zbuf[1, pl.ds(at, BX), :] = res[BX:]
        return carry

    lax.fori_loop(0, LEV // 2, local_y, 0)

    for cp in ycp:
        cp.wait()
    zero = jnp.zeros((GROUPS, 128), F32)
    sa = sb = la = lh = zero
    for d in range(3):
        from_left = (yy - (d + 1)) >= 0
        u, w = yrcv[d, 0], yrcv[d, 1]
        sa = sa + jnp.where(from_left, u, 0.0)
        sb = sb + jnp.where(from_left, w, 0.0)
        la = la + jnp.where(from_left, 0.0, u)
        lh = lh + jnp.where(from_left, 0.0, w)
    zsnd[0] = sa + jnp.where(hh == 0, own_y[0], 0.0)
    zsnd[1] = sb + jnp.where(hh == 0, own_y[1], 0.0)
    zsnd[2] = la + jnp.where(hh == 1, own_y[2], 0.0)
    zsnd[3] = lh + jnp.where(hh == 1, own_y[3], 0.0)
    hcp = pltpu.make_async_remote_copy(
        src_ref=zsnd, dst_ref=zrcv, send_sem=h_s, recv_sem=h_r, device_id=across, device_id_type=MESH)
    hcp.start()
    lax.fori_loop(LEV // 2, LEV, local_y, 0)
    lx = Line(lx_rate, NX, BX, gx)
    hcp.wait()
    sa = sa + zrcv[0]
    sb = sb + zrcv[1]
    la = la + zrcv[2]
    lh = lh + zrcv[3]
    k1 = (ly.p_n2 * (sb - sa * (ly.n2 + ly.G)) + ly.p_inv * (la - lh * ly.last)
          + ly.ga * ly.p_inv * (ly.p_s * q1)
          - ly.p_n2 * ly.p_inv * ((2.0 * (NY - ly.last) + ly.G) * r1 + r2))
    k2 = lh * ly.p_inv - sa * ly.p_n2 - ly.p_n2 * ly.p_inv * r1
    k3 = ly.p_s * (sa * (ly.s + ly.G) - sb - lh * ly.g + ly.ga * ly.p_inv * r1 - ly.g * ly.p_s * q1)
    k4 = sa * ly.p_s
    for q, k in enumerate((k1, k2, k3, k4, zero, zero, zero, zero)):
        kap[pl.ds(q, GROUPS, stride=8), :] = k

    def synth(g, carry):
        at = pl.multiple_of(g * 64, 64)
        k8 = kap[pl.ds(pl.multiple_of(g * 8, 8), 8), :]
        lane = (iota((8, 128), 1) // BX) % 4
        big = jnp.concatenate([jnp.where(lane == lv, k8, 0.0) for lv in range(4)], axis=0)
        kh, kl = split(big.T)
        wh, wl = split(wtab[pl.ds(pl.multiple_of(g * 32, 32), 32), :])
        res = dot(kh, wh, NN) + dot(kl, wh, NN) + dot(kh, wl, NN)
        zbuf[0, pl.ds(at, 64), :] += res[0:64]
        zbuf[1, pl.ds(at, 64), :] += res[64:]
        return carry

    lax.fori_loop(0, GROUPS, synth, 0)

    a_sub = lx.a

    def x_moments(k):
        r1 = jnp.zeros((LEV, 128), F32)
        r2, q1, q2 = r1, r1, r1
        for x in range(BX):
            v = zbuf[k, pl.ds(x, LEV, stride=BX), :]
            t = a_sub * r1
            r2 = a_sub * r2 + t
            r1 = t + v
            v = zbuf[k, pl.ds(BX - 1 - x, LEV, stride=BX), :]
            t = a_sub * q1
            q2 = a_sub * q2 + t
            q1 = t + v
        return lx.sums(r1, r2, q1, q2)

    for k in range(KLOC):
        for q, s in enumerate(x_moments(k)):
            xst[k, q] = s
    pcp = pltpu.make_async_remote_copy(
        src_ref=xst.at[1 - core], dst_ref=xpair, send_sem=p_s, recv_sem=p_r, device_id=sibling, device_id_type=MESH)
    pcp.start()
    pcp.wait()

    def chain(turn):
        way = ((z >= 4).astype(jnp.int32) + turn) % 2
        has_in = jnp.where(way == 0, z > 0, z < 7)
        has_out = jnp.where(way == 0, z < 7, z > 0)
        target = (i, gx + 2 - 4 * way, gy)
        part = pl.multiple_of(way * 2, 2)

        def copy(c):
            rows = pl.ds(c * CHUNK, CHUNK)
            return pltpu.make_async_remote_copy(
                src_ref=xout.at[way, :, rows], dst_ref=xin.at[way, :, rows],
                send_sem=c_s.at[way, c], recv_sem=c_r.at[way, c], device_id=target, device_id_type=MESH)

        @pl.when(jnp.logical_not(has_in))
        def _():
            xin[way] = jnp.zeros((2, LEV, 128), F32)

        for c in range(CHUNKS):
            rows = slice(c * CHUNK, (c + 1) * CHUNK)

            @pl.when(has_in)
            def _():
                copy(c).wait_recv()

            @pl.when(has_out)
            def _():
                xout[way, :, rows] = (xin[way, :, rows] + xst[core, pl.ds(part, 2), rows]
                                      + xpair[pl.ds(part, 2), rows])
                copy(c).start()

        add = jnp.where(way == core, 1.0, 0.0)
        xss[way] = xin[way] + add * xst[core, pl.ds(part, 2)]
        sib = pltpu.make_async_remote_copy(
            src_ref=xss.at[way], dst_ref=xsr.at[way], send_sem=d_s.at[way], recv_sem=d_r.at[way],
            device_id=sibling, device_id_type=MESH)
        sib.start()
        xin[way] = xin[way] + (1.0 - add) * xpair[pl.ds(part, 2)]
        return way, has_out, copy, sib

    done = [chain(0), chain(1)]
    for way, has_out, copy, sib in done:
        for c in range(CHUNKS):
            @pl.when(has_out)
            def _():
                copy(c).wait_send()
    for way, has_out, copy, sib in done:
        sib.wait()

    g, ga, s, e, G = lx.g, lx.ga, lx.s, lx.e, lx.G
    ge = 1.0 + g
    p_e, p_me, p_2e = lx.power(e), lx.power(-e), lx.power(2.0 * NX - e)
    hx = p_e - p_2e
    ux = p_e * (e + G) - p_2e * (2.0 * NX - e + G)
    p_s1, p_ms1 = lx.power(s - 1.0), lx.power(-s - 1.0)
    c2a = s + g + ga - g * lx.power(2.0 * NX - 2.0 * s)
    c2h = g * (p_ms1 - p_s1)
    mine = core == 0

    for k in range(KLOC):
        local = core == k
        sa = jnp.where(local, xin[0, 0], xsr[0, 0])
        sb = jnp.where(local, xin[0, 1], xsr[0, 1])
        la = jnp.where(local, xin[1, 0], xsr[1, 0])
        lh = jnp.where(local, xin[1, 1], xsr[1, 1])
        oa, ob, _, oh = xst[k, 0], xst[k, 1], xst[k, 2], xst[k, 3]
        c1 = p_s1 * sa
        d1 = ge * (hx * (sa + oa) + p_me * lh)
        c2 = ge * (p_s1 * (c2a * sa - sb) + c2h * (oh + lh))
        d2 = ge * ge * (ux * (sa + oa) - hx * (sb + ob) + p_me * la - (e * p_me + g * p_e) * lh)
        for t in range(LEV // 8):
            lo = t * 8
            a8 = a_sub[lo:lo + 8]
            line = [zbuf[k, pl.ds(lo * BX + x, 8, stride=BX), :] for x in range(BX)]
            for carry, order in ((c1, 1), (d1, -1), (c2, 1), (d2, -1)):
                run = carry[lo:lo + 8]
                for x in range(BX)[::order]:
                    run = a8 * run + line[x]
                    line[x] = run
            for x in range(BX):
                fbuf[k, x, lo:lo + 8, :] = line[x]

    alpha = lx_rate / (1.0 + a_sub)
    scale = 2.0 * lx_rate * lx_rate * lx_rate * alpha * alpha
    pid = iota((LEV, LEV), 0)
    lid = iota((LEV, LEV), 1)
    keep = jnp.abs(pid - lid) <= bands[...]
    mixed = jnp.where(keep, weights[...], 0.0) * scale[:, 0:LEV]
    mh, ml = split(mixed.T)
    mcat = jnp.concatenate([mh, mh, ml], axis=1)
    loads[2].wait()

    def mix(x, carry):
        for k in range(KLOC):
            fh, fl = split(fbuf[k, x])
            fcat = jnp.concatenate([fh, fl, fh], axis=0)
            out_v[k, pl.ds(x, LEV, stride=BX), :] = dot(mcat, fcat, NN)
        return carry

    lax.fori_loop(0, BX, mix, 0, unroll=2)
    stores = []
    for k in range(KLOC):
        out_v[k] = out_v[k] + ctl_v[k].astype(F32)
        cp = pltpu.make_async_copy(out_v.at[k], out.at[k], in_sem.at[3 + k])
        cp.start()
        stores.append(cp)
    for cp in stores:
        cp.wait()


def per_device(members, gradient, control, filter_rates, vertical_weights, band_widths):
    any_ = pl.BlockSpec(memory_space=pl.ANY)
    vm = pl.BlockSpec(memory_space=pltpu.VMEM)
    dma = pltpu.SemaphoreType.DMA
    out = pl.pallas_call(
        kernel,
        out_shape=jax.ShapeDtypeStruct((KLOC, ROWS, BY), F32),
        in_specs=[pl.BlockSpec(memory_space=pltpu.SMEM), vm, vm, vm, any_, any_, any_],
        out_specs=any_,
        scratch_shapes=[
            pltpu.VMEM((KLOC, ROWS, BY), BF16),
            pltpu.VMEM((ROWS, BY), F32),
            pltpu.VMEM((KLOC, ROWS, BY), BF16),
            pltpu.VMEM((KLOC, ROWS, BY), F32),
            pltpu.VMEM((ROWS, BY), F32),
            pltpu.VMEM((ROWS, BY), F32),
            pltpu.VMEM((3, QUARTER, BY), F32),
            pltpu.VMEM((KLOC, ROWS, BY), F32),
            pltpu.VMEM((KLOC, ROWS, BY), F32),
            pltpu.VMEM((LEV * 8, 128), F32),
            pltpu.VMEM((LEV, 128), F32),
            pltpu.VMEM((LEV * BY, BY), BF16),
            pltpu.VMEM((LEV * BY, BY), BF16),
            pltpu.VMEM((GROUPS * 8, 128), F32),
            pltpu.VMEM((4, GROUPS, 128), F32),
            pltpu.VMEM((3, 2, GROUPS, 128), F32),
            pltpu.VMEM((4, GROUPS, 128), F32),
            pltpu.VMEM((4, GROUPS, 128), F32),
            pltpu.VMEM((GROUPS * 8, 128), F32),
            pltpu.VMEM((KLOC, 4, LEV, 128), F32),
            pltpu.VMEM((4, LEV, 128), F32),
            pltpu.VMEM((2, 2, LEV, 128), F32),
            pltpu.VMEM((2, 2, LEV, 128), F32),
            pltpu.VMEM((2, 2, LEV, 128), F32),
            pltpu.VMEM((2, 2, LEV, 128), F32),
            pltpu.VMEM((KLOC, BX, LEV, BY), F32),
            dma((5,)),
            dma((3,)), dma((3,)), dma((3,)), dma((3,)), dma((3,)), dma((3,)),
            dma, dma, dma, dma,
            dma((2, CHUNKS)), dma((2, CHUNKS)), dma((2,)), dma((2,)),
        ],
        compiler_params=pltpu.CompilerParams(
            collective_id=0, has_side_effects=True, vmem_limit_bytes=44 << 20),
        name="localize",
    )(
        filter_rates, filter_rates.reshape(1, LEV), band_widths.reshape(1, LEV), vertical_weights,
        members.reshape(KLOC, ROWS, BY), gradient.reshape(ROWS, BY), control.reshape(KLOC, ROWS, BY),
    )
    return out.reshape(KLOC, LEV, BX, BY)


def solution(mesh):
    placed = (
        P("mem", None, "gx", "gy"),
        P(None, "gx", "gy"),
        P("mem", None, "gx", "gy"),
        P(),
        P(),
        P(),
    )
    return jax.shard_map(
        per_device,
        mesh=mesh,
        in_specs=placed,
        out_specs=P("mem", None, "gx", "gy"),
        check_vma=False,
    )
```

```python
import functools

import jax
import jax.numpy as jnp
from jax import lax
from jax.experimental import pallas as pl
from jax.experimental.pallas import tpu as pltpu
from jax.sharding import PartitionSpec as P

MESH = pl.DeviceIdType.MESH
F32 = jnp.float32
BF16 = jnp.bfloat16

LEV, MEMBERS, NX, NY = 64, 8, 256, 1024
MEM, GX, GY = 4, 16, 8
KLOC = MEMBERS // MEM
BX, BY = NX // GX, NY // GY
ROWS = LEV * BX
GROUPS = LEV // 4
QUARTER = ROWS // MEM
CHUNKS = 4
CHUNK = LEV // CHUNKS
T1, T2 = 16, 32

NT = (((1,), (1,)), ((), ()))
NN = (((1,), (0,)), ((), ()))
TN = (((0,), (0,)), ((), ()))


def dot(a, b, dims):
    return lax.dot_general(a, b, dims, preferred_element_type=F32)


def split(x):
    hi = x.astype(BF16)
    return hi, (x - hi.astype(F32)).astype(BF16)


def iota(shape, axis):
    return lax.broadcasted_iota(jnp.int32, shape, axis)


def log_decay(r):
    return -r * (1.0 + r * (0.5 + r * (1.0 / 3 + r * (0.25 + r * (0.2 + r * (1.0 / 6))))))


class Line:
    def __init__(self, rate, total, size, index):
        r = rate
        self.rate = r
        self.log = log_decay(r)
        self.a = 1.0 - r
        self.g = self.a * self.a / (r * (1.0 + self.a))
        self.s = (index * size).astype(F32)
        self.last = self.s + (size - 1.0)
        self.n2 = 2.0 * total - self.last
        self.p_s = self.power(self.s)
        self.p_inv = self.power(-self.last)
        self.p_n2 = self.power(self.n2)
        self.ga = self.g * self.power(2.0 * total)
        self.G = 1.0 + 2.0 * self.g + self.ga
        self.total = total
        self.e = self.s + size

    def reach(self, t):
        near = t + self.g + self.ga - self.g * self.power(2.0 * (self.total - t))
        far = self.g * (self.power(-t - 1.0) - self.power(t - 1.0))
        return near, far

    def power(self, m):
        return jnp.exp(self.log * m)

    def sums(self, r1, r2, q1, q2):
        sa = self.p_inv * r1
        fq = self.p_s * q1
        sb = self.p_inv * (self.last * r1 - r2) + self.g * fq
        lh = fq - self.p_n2 * r1
        la = self.p_s * ((self.s + self.G) * q1 + q2) - self.p_n2 * ((self.n2 + self.G) * r1 + r2)
        return sa, sb, la, lh


def kernel(rates_h, bands_h, weights_h, members, gradient, control, out,
           rates, bands, weights, mem_v, grad_v, ctl_v, psum, total, rs_rcv, vbuf, zbuf, wtab, lsub, thi, tlo,
           mu, ysum, yone, xsum, xrs, xmn, ysnd, yrcv, zsnd, zrcv, kap, xst, xpair, xin, xout, xss, xsr,
           cown, csib, ctot, crcv, xr, xf, fbuf,
           in_sem, rs_s, rs_r, ag_s, ag_r, o_s, o_r, xs_s, xs_r, xa_s, xa_r, y_s, y_r, h_s, h_r, p_s, p_r,
           c_s, c_r, d_s, d_r, k_s, k_r, l_s, l_r):
    i = lax.axis_index("mem")
    gx = lax.axis_index("gx")
    gy = lax.axis_index("gy")
    z, core = gx // 2, gx % 2
    yy, hh = gy // 2, gy % 2

    barrier = pltpu.get_barrier_semaphore()

    def signal(dev):
        pl.semaphore_signal(barrier, inc=1, device_id=dev, device_id_type=MESH)

    sibling = (i, gx + 1 - 2 * core, gy)
    across = (i, gx, gy + 1 - 2 * hh)
    peers = [((i + d) % MEM, gx, gy) for d in range(1, MEM)]
    y_at = [(yy + d) % 4 for d in range(1, 4)]
    chips = [(i, ((z + d) % 8) * 2 + core, gy) for d in range(1, 8)]
    signal(across)
    for dev in chips[2:5] + chips[1:2] + chips[5:6] + chips[0:1] + chips[6:7]:
        signal(dev)
    for d in range(3):
        signal(peers[d])
        signal((i, gx, y_at[d] * 2 + hh))
    signal(sibling)

    loads = [
        pltpu.make_async_copy(rates_h, rates, in_sem.at[0]),
        pltpu.make_async_copy(members, mem_v, in_sem.at[1]),
        pltpu.make_async_copy(gradient, grad_v, in_sem.at[2]),
        pltpu.make_async_copy(weights_h, weights, in_sem.at[3]),
        pltpu.make_async_copy(bands_h, bands, in_sem.at[4]),
        pltpu.make_async_copy(control, ctl_v, in_sem.at[5]),
    ]
    for load in loads:
        load.start()

    def remote(src, dst, ss, rs, dev):
        return pltpu.make_async_remote_copy(
            src_ref=src, dst_ref=dst, send_sem=ss, recv_sem=rs, device_id=dev, device_id_type=MESH)

    loads[0].wait()
    sub8 = iota((8, 128), 0)
    for t in range(LEV // 8):
        v = jnp.zeros((8, 128), F32)
        for j in range(8):
            v = jnp.where(sub8 == j, rates[t * 8 + j], v)
        lsub[t * 8:(t + 1) * 8, :] = v
    lane = iota((GROUPS, 128), 1)
    lev_id = iota((GROUPS, 128), 0) * 4 + (lane // BX) % 4
    rate_lane = jnp.zeros((GROUPS, 128), F32)
    for l in range(LEV):
        rate_lane = jnp.where(lev_id == l, rates[l], rate_lane)
    ly = Line(rate_lane, NY, BY, gy)
    lx = Line(lsub[...], NX, BX, gx)
    a_sub = lx.a

    cell = iota((8, 128), 1).astype(F32)
    kind = sub8 % 4
    dist = jnp.where(kind < 2, 127.0 - cell, cell)
    factor = jnp.where(kind % 2 == 0, 1.0, dist)

    def basis(l, carry):
        lg = log_decay(jnp.broadcast_to(lsub[pl.ds(l, 1), :], (8, 128)))
        wtab[pl.ds(pl.multiple_of(l * 8, 8), 8), :] = jnp.exp(dist * lg) * factor
        return carry

    lax.fori_loop(0, LEV, basis, 0, unroll=8)

    loads[1].wait()
    loads[2].wait()
    lane8 = (iota((8, 128), 1) // BX) % 4

    def product(g, carry):
        at = pl.multiple_of(g * 64, 64)
        gr = grad_v[pl.ds(at, 64), :]
        m0 = mem_v[0, pl.ds(at, 64), :].astype(F32)
        m1 = mem_v[1, pl.ds(at, 64), :].astype(F32)
        psum[pl.ds(at, 64), :] = m0 + m1
        v0 = m0 * gr
        v1 = m1 * gr
        vbuf[0, pl.ds(at, 64), :] = v0
        vbuf[1, pl.ds(at, 64), :] = v1
        vh, vl = split(jnp.concatenate([v0, v1], axis=0))
        wh, wl = split(wtab[pl.ds(pl.multiple_of(g * 32, 32), 32), :])
        res = dot(wh, vh, NT) + dot(wh, vl, NT) + dot(wl, vh, NT)
        m8 = jnp.zeros((8, 128), F32)
        for lv in range(4):
            m8 = jnp.where(lane8 == lv, res[lv * 8:lv * 8 + 8, :], m8)
        mu[pl.ds(pl.multiple_of(g * 8, 8), 8), :] = m8
        return carry

    lax.fori_loop(0, GROUPS, product, 0, unroll=2)
    ymom = [mu[pl.ds(q, GROUPS, stride=8), :] for q in range(4)]
    low = lane < 64
    two = [m + pltpu.roll(m, 64, 1) for m in ymom]
    ysum[0] = jnp.where(low, two[0], two[1])
    ysum[1] = jnp.where(low, two[2], two[3])

    pl.semaphore_wait(barrier, 15)
    one = [remote(ysum, yone.at[d], o_s.at[d], o_r.at[d], peers[d]) for d in range(3)]
    for cp in one:
        cp.start()

    for k in range(KLOC):
        r1 = jnp.zeros((LEV, 128), F32)
        r2, q1, q2 = r1, r1, r1
        for x in range(BX):
            v = vbuf[k, pl.ds(x, LEV, stride=BX), :]
            t = a_sub * r1
            r2 = a_sub * r2 + t
            r1 = t + v
            v = vbuf[k, pl.ds(BX - 1 - x, LEV, stride=BX), :]
            t = a_sub * q1
            q2 = a_sub * q2 + t
            q1 = t + v
        for q, s in enumerate(lx.sums(r1, r2, q1, q2)):
            xst[k, q] = s
            if k == 1:
                xsum[q] = xst[0, q] + s
    own16 = pl.multiple_of(i * 16, 16)
    xrc = [remote(xsum.at[:, pl.ds(pl.multiple_of(peers[d][0] * 16, 16), 16)], xrs.at[d],
                  xs_s.at[d], xs_r.at[d], peers[d]) for d in range(3)]
    for cp in xrc:
        cp.start()
    rs = [remote(psum.at[pl.ds(pl.multiple_of(peers[d][0] * QUARTER, QUARTER), QUARTER)], rs_rcv.at[d],
                 rs_s.at[d], rs_r.at[d], peers[d]) for d in range(3)]
    for cp in rs:
        cp.start()

    di = jnp.abs(iota((BY, BY), 0) - iota((BY, BY), 1)).astype(F32)

    def toeplitz(l, carry):
        r = jnp.broadcast_to(lsub[pl.ds(l, 1), :], (8, 128))
        lg = log_decay(r)
        a = 1.0 - r
        c = 1.0 + 2.0 * (a * a / (r * (1.0 + a)))
        lg = jnp.broadcast_to(lg[0:1, :], (BY, BY))
        c = jnp.broadcast_to(c[0:1, :], (BY, BY))
        hi, lo = split(jnp.exp(di * lg) * (di + c))
        at = pl.multiple_of(l * BY, BY)
        thi[pl.ds(at, BY), :] = hi
        tlo[pl.ds(at, BY), :] = lo
        return carry

    lax.fori_loop(0, T1, toeplitz, 0)

    for cp in one:
        cp.wait()
    tot = [ysum[j] + yone[0, j] + yone[1, j] + yone[2, j] for j in range(2)]
    swap = [pltpu.roll(t, 64, 1) for t in tot]
    mean = [jnp.where(low, tot[0], swap[0]), jnp.where(low, swap[0], tot[0]),
            jnp.where(low, tot[1], swap[1]), jnp.where(low, swap[1], tot[1])]
    r1, r2, q1, q2 = [m - t * (1.0 / MEMBERS) for m, t in zip(ymom, mean)]
    own_y = ly.sums(r1, r2, q1, q2)
    for q in range(4):
        ysnd[q] = own_y[q]
    ycp = []
    for d in range(3):
        part = pl.multiple_of(jnp.where(y_at[d] > yy, 0, 2), 2)
        cp = remote(ysnd.at[pl.ds(part, 2)], yrcv.at[d], y_s.at[d], y_r.at[d], (i, gx, y_at[d] * 2 + hh))
        cp.start()
        ycp.append(cp)

    for cp in xrc:
        cp.wait()
    xmn[:, pl.ds(own16, 16)] = (xsum[:, pl.ds(own16, 16)] + xrs[0] + xrs[1] + xrs[2]) * (1.0 / MEMBERS)
    xag = [remote(xmn.at[:, pl.ds(own16, 16)], xmn.at[:, pl.ds(own16, 16)], xa_s.at[d], xa_r.at[d], peers[d])
           for d in range(3)]
    for cp in xag:
        cp.start()
    lax.fori_loop(T1, T2, toeplitz, 0)

    for cp in ycp:
        cp.wait()
    zero = jnp.zeros((GROUPS, 128), F32)
    sa = sb = la = lh = zero
    for d in range(3):
        from_left = (yy - (d + 1)) >= 0
        u, w = yrcv[d, 0], yrcv[d, 1]
        sa = sa + jnp.where(from_left, u, 0.0)
        sb = sb + jnp.where(from_left, w, 0.0)
        la = la + jnp.where(from_left, 0.0, u)
        lh = lh + jnp.where(from_left, 0.0, w)
    zsnd[0] = sa + jnp.where(hh == 0, own_y[0], 0.0)
    zsnd[1] = sb + jnp.where(hh == 0, own_y[1], 0.0)
    zsnd[2] = la + jnp.where(hh == 1, own_y[2], 0.0)
    zsnd[3] = lh + jnp.where(hh == 1, own_y[3], 0.0)
    hcp = remote(zsnd, zrcv, h_s, h_r, across)
    hcp.start()

    for cp in xag:
        cp.wait()
    for k in range(KLOC):
        xst[k] = xst[k] - xmn[...]
    pcp = remote(xst.at[1 - core], xpair, p_s, p_r, sibling)
    pcp.start()

    own = pl.multiple_of(i * QUARTER, QUARTER)
    for cp in rs:
        cp.wait()
    total[pl.ds(own, QUARTER), :] = (psum[pl.ds(own, QUARTER), :] + rs_rcv[0]
                                     + rs_rcv[1] + rs_rcv[2])
    ag = [remote(total.at[pl.ds(own, QUARTER)], total.at[pl.ds(own, QUARTER)], ag_s.at[d], ag_r.at[d], peers[d])
          for d in range(3)]
    for cp in ag:
        cp.start()
    pcp.wait()

    def chain(turn):
        way = ((z >= 4).astype(jnp.int32) + turn) % 2
        has_in = jnp.where(way == 0, z > 0, z < 7)
        has_out = jnp.where(way == 0, z < 7, z > 0)
        target = (i, gx + 2 - 4 * way, gy)
        part = pl.multiple_of(way * 2, 2)

        def copy(c):
            rows = pl.ds(c * CHUNK, CHUNK)
            return remote(xout.at[way, :, rows], xin.at[way, :, rows], c_s.at[way, c], c_r.at[way, c], target)

        @pl.when(jnp.logical_not(has_in))
        def _():
            xin[way] = jnp.zeros((2, LEV, 128), F32)

        for c in range(CHUNKS):
            rows = slice(c * CHUNK, (c + 1) * CHUNK)

            @pl.when(has_in)
            def _():
                copy(c).wait_recv()

            @pl.when(has_out)
            def _():
                xout[way, :, rows] = (xin[way, :, rows] + xst[core, pl.ds(part, 2), rows]
                                      + xpair[pl.ds(part, 2), rows])
                copy(c).start()

        add = jnp.where(way == core, 1.0, 0.0)
        xss[way] = xin[way] + add * xst[core, pl.ds(part, 2)]
        sib = remote(xss.at[way], xsr.at[way], d_s.at[way], d_r.at[way], sibling)
        sib.start()
        xin[way] = xin[way] + (1.0 - add) * xpair[pl.ds(part, 2)]
        return way, has_out, copy, sib

    def drain(done):
        for way, has_out, copy, sib in done:
            sib.wait()
            for c in range(CHUNKS):
                @pl.when(has_out)
                def _():
                    copy(c).wait_send()

    done = [chain(0)]

    hcp.wait()
    sa = sa + zrcv[0]
    sb = sb + zrcv[1]
    la = la + zrcv[2]
    lh = lh + zrcv[3]
    k1 = (ly.p_n2 * (sb - sa * (ly.n2 + ly.G)) + ly.p_inv * (la - lh * ly.last)
          + ly.ga * ly.p_inv * (ly.p_s * q1)
          - ly.p_n2 * ly.p_inv * ((2.0 * (NY - ly.last) + ly.G) * r1 + r2))
    k2 = lh * ly.p_inv - sa * ly.p_n2 - ly.p_n2 * ly.p_inv * r1
    k3 = ly.p_s * (sa * (ly.s + ly.G) - sb - lh * ly.g + ly.ga * ly.p_inv * r1 - ly.g * ly.p_s * q1)
    k4 = sa * ly.p_s
    kk = (k1, k2, k3, k4)

    lxl = Line(rate_lane, NX, BX, gx)
    xc = (lane % BX).astype(F32)
    up, down = lxl.power(xc), lxl.power(BX - 1.0 - xc)
    wts = lxl.sums(down, (BX - 1.0 - xc) * down, up, xc * up)
    stack = jnp.concatenate([w * kq for w in wts for kq in kk], axis=0)
    seg = (iota((128, 128), 0) // BX == iota((128, 128), 1) // BX).astype(BF16)
    sh, sl = split(stack)
    res = dot(sh, seg, NN) + dot(sl, seg, NN)
    slot = lane % BX
    cor = zero
    for c in range(16):
        cor = jnp.where(slot == c, res[c * GROUPS:(c + 1) * GROUPS], cor)
    cown[...] = cor
    lcp = remote(cown, csib, l_s, l_r, sibling)
    lcp.start()
    for q, k in enumerate(kk + (zero,) * 4):
        kap[pl.ds(q, GROUPS, stride=8), :] = k
    lcp.wait()
    ctot[...] = cor + csib[...]
    ccp = [remote(ctot, crcv.at[d], k_s.at[d], k_r.at[d], chips[d]) for d in range(7)]
    for d in (3, 2, 4, 1, 5, 0, 6):
        ccp[d].start()

    def local_y(l, carry):
        at = pl.multiple_of(l * BX, BX)
        tt = pl.multiple_of(l * BY, BY)
        mean = total[pl.ds(at, BX), :] * (1.0 / MEMBERS)
        gr = grad_v[pl.ds(at, BX), :]
        v = jnp.concatenate([(mem_v[k, pl.ds(at, BX), :].astype(F32) - mean) * gr for k in range(KLOC)], axis=0)
        vh, vl = split(v)
        th = thi[pl.ds(tt, BY), :]
        res = dot(vh, th, NN) + dot(vl, th, NN) + dot(vh, tlo[pl.ds(tt, BY), :], NN)
        zbuf[0, pl.ds(at, BX), :] = res[0:BX]
        zbuf[1, pl.ds(at, BX), :] = res[BX:]
        return carry

    def synth(g, carry):
        at = pl.multiple_of(g * 64, 64)
        k8 = kap[pl.ds(pl.multiple_of(g * 8, 8), 8), :]
        big = jnp.concatenate([jnp.where(lane8 == lv, k8, 0.0) for lv in range(4)], axis=0)
        kh, kl = split(big.T)
        wh, wl = split(wtab[pl.ds(pl.multiple_of(g * 32, 32), 32), :])
        res = dot(kh, wh, NN) + dot(kl, wh, NN) + dot(kh, wl, NN)
        zbuf[0, pl.ds(at, 64), :] += res[0:64]
        zbuf[1, pl.ds(at, 64), :] += res[64:]
        return carry

    def block():
        for cp in ag:
            cp.wait()
        lax.fori_loop(0, LEV, local_y, 0, unroll=2)
        lax.fori_loop(0, GROUPS, synth, 0)

    middle = (z == 3) | (z == 4)
    for load in loads[3:5]:
        load.wait()
    alpha = lx.rate / (1.0 + a_sub)
    scale = 2.0 * lx.rate * lx.rate * lx.rate * alpha * alpha
    pid = iota((LEV, LEV), 0)
    lid = iota((LEV, LEV), 1)
    keep = jnp.abs(pid - lid) <= bands[...]
    mixed = jnp.where(keep, weights[...], 0.0) * scale[:, 0:LEV]
    mh, ml = split(mixed.T)
    mcat = jnp.concatenate([mh, mh, ml], axis=1)

    def rest():
        lax.fori_loop(T2, LEV, toeplitz, 0)
        block()

    @pl.when(jnp.logical_not(middle))
    def _():
        rest()

    done.append(chain(1))

    @pl.when(middle)
    def _():
        rest()

    drain(done)

    for k in range(KLOC):
        for q in range(4):
            row = (k * 4 + q) * LEV
            xr[row:row + LEV, :] = jnp.where(core == k, xin[q // 2, q % 2], xsr[q // 2, q % 2])

    def local_x(l, carry):
        tt = pl.multiple_of(l * BY, BY)
        vh, vl = split(xr[pl.ds(l, 8, stride=LEV), :])
        th = thi[pl.ds(tt, BY), :]
        xf[pl.ds(l, 8, stride=LEV), :] = dot(vh, th, NN) + dot(vl, th, NN) + dot(vh, tlo[pl.ds(tt, BY), :], NN)
        return carry

    lax.fori_loop(0, LEV, local_x, 0, unroll=4)
    for cp in ccp:
        cp.wait()
    right = slot < 8
    cst = jnp.where(right == (core == 1), csib[...], 0.0)
    for d in range(7):
        from_left = (z - (d + 1)) >= 0
        cst = cst + jnp.where(right == from_left, crcv[d], 0.0)
    cown[...] = cst
    zr, zc = iota((64, 256), 0), iota((64, 256), 1)
    fits = ((zr // 32 == (zc // 64) % 2) & ((zr // 8) % 4 == (zc // 4) % 4)
            & ((zr % 8) // 4 == zc // 128) & (zr % 4 == (zc // 16) % 4))

    def synth_x(t, carry):
        row = jnp.concatenate([cown[pl.ds(2 * t, 1), :], cown[pl.ds(2 * t + 1, 1), :]], axis=1)
        kh, kl = split(jnp.where(fits, jnp.broadcast_to(row, (64, 256)), 0.0))
        w = wtab[pl.ds(pl.multiple_of(t * 64, 64), 64), :]
        tiles = [w[(g * 4 + lv) * 8:(g * 4 + lv) * 8 + 8] for g in range(2) for k in range(2)
                 for lv in range(4) for twice in range(2)]
        wh, wl = split(jnp.concatenate(tiles, axis=0))
        res = dot(kh, wh, NN) + dot(kl, wh, NN) + dot(kh, wl, NN)
        for j in range(8):
            xf[pl.ds(pl.multiple_of(j * LEV + t * 8, 8), 8), :] += res[j * 8:(j + 1) * 8]
        return carry

    lax.fori_loop(0, LEV // 8, synth_x, 0)

    g, s, e, G = lx.g, lx.s, lx.e, lx.G
    ge = 1.0 + g
    p_s, p_e, p_me, p_2e = lx.power(s), lx.power(e), lx.power(-e), lx.power(2.0 * NX - e)
    hx = p_e - p_2e
    ux = p_e * (e + G) - p_2e * (2.0 * NX - e + G)
    hs = p_s - lx.power(2.0 * NX - s)
    p_s1, p_1e = lx.power(s - 1.0), lx.power(1.0 - e)
    near_s, far_s = lx.reach(s)
    near_e, far_e = lx.reach(e)

    for k in range(KLOC):
        for t in range(LEV // 8):
            lo = t * 8
            cut = lambda m: m[lo:lo + 8]
            sa, sb, la, lh = [xf[(k * 4 + q) * LEV + lo:(k * 4 + q) * LEV + lo + 8, :] for q in range(4)]
            a8, ge8, hx8, pm8 = cut(a_sub), cut(ge), cut(hx), cut(p_me)
            line = [zbuf[k, pl.ds(lo * BX + x, 8, stride=BX), :] for x in range(BX)]

            def sweep(run, order):
                for x in range(BX)[::order]:
                    run = a8 * run + line[x]
                    line[x] = run
                return run

            sa_e = cut(p_1e) * sweep(cut(p_s1) * sa, 1)
            first = sweep(ge8 * (hx8 * sa_e + pm8 * lh), -1)
            lh_s = cut(p_s) * (first / ge8 - cut(hs) * sa)
            last = sweep(ge8 * (cut(p_s1) * (cut(near_s) * sa - sb) + cut(far_s) * lh_s), 1)
            sb_e = cut(near_e) * sa_e - cut(p_1e) * (last / ge8 - cut(far_e) * lh)
            sweep(ge8 * ge8 * (cut(ux) * sa_e - hx8 * sb_e + pm8 * la - (e * pm8 + cut(g) * cut(p_e)) * lh), -1)
            for x in range(BX):
                fbuf[k, x, lo:lo + 8, :] = line[x]

    def mix(x, carry):
        for k in range(KLOC):
            fh, fl = split(fbuf[k, x])
            fcat = jnp.concatenate([fh, fl, fh], axis=0)
            out[k, pl.ds(x, LEV, stride=BX), :] = dot(mcat, fcat, NN)
        return carry

    lax.fori_loop(0, BX, mix, 0, unroll=2)
    loads[5].wait()
    for k in range(KLOC):
        out[k] = out[k] + ctl_v[k].astype(F32)


def per_device(members, gradient, control, filter_rates, vertical_weights, band_widths):
    hbm = pl.BlockSpec(memory_space=pltpu.HBM)
    dma = pltpu.SemaphoreType.DMA

    def vm(*shape):
        return pltpu.VMEM(shape, F32)

    three = [dma((3,))] * 2
    single = [dma] * 2
    out = pl.pallas_call(
        kernel,
        out_shape=jax.ShapeDtypeStruct((KLOC, ROWS, BY), F32),
        in_specs=[hbm] * 6,
        out_specs=pl.BlockSpec(memory_space=pltpu.VMEM),
        scratch_shapes=[
            pltpu.SMEM((LEV,), F32),
            pltpu.VMEM((1, LEV), jnp.int32),
            vm(LEV, LEV),
            pltpu.VMEM((KLOC, ROWS, BY), BF16),
            vm(ROWS, BY),
            pltpu.VMEM((KLOC, ROWS, BY), BF16),
            vm(ROWS, BY), vm(ROWS, BY), vm(3, QUARTER, BY),
            vm(KLOC, ROWS, BY), vm(KLOC, ROWS, BY),
            vm(LEV * 8, 128), vm(LEV, 128),
            pltpu.VMEM((LEV * BY, BY), BF16),
            pltpu.VMEM((LEV * BY, BY), BF16),
            vm(GROUPS * 8, 128),
            vm(2, GROUPS, 128), vm(3, 2, GROUPS, 128),
            vm(4, LEV, 128), vm(3, 4, 16, 128), vm(4, LEV, 128),
            vm(4, GROUPS, 128), vm(3, 2, GROUPS, 128), vm(4, GROUPS, 128), vm(4, GROUPS, 128),
            vm(GROUPS * 8, 128),
            vm(KLOC, 4, LEV, 128), vm(4, LEV, 128),
            vm(2, 2, LEV, 128), vm(2, 2, LEV, 128), vm(2, 2, LEV, 128), vm(2, 2, LEV, 128),
            vm(GROUPS, 128), vm(GROUPS, 128), vm(GROUPS, 128), vm(7, GROUPS, 128),
            vm(8 * LEV, 128), vm(8 * LEV, 128),
            vm(KLOC, BX, LEV, BY),
            dma((6,)),
            *three, *three, *three, *three, *three, *three,
            *single, *single,
            dma((2, CHUNKS)), dma((2, CHUNKS)), dma((2,)), dma((2,)),
            dma((7,)), dma((7,)), *single,
        ],
        compiler_params=pltpu.CompilerParams(
            collective_id=0, has_side_effects=True, vmem_limit_bytes=60 << 20),
        name="localize",
    )(
        filter_rates, band_widths.reshape(1, LEV), vertical_weights,
        members.reshape(KLOC, ROWS, BY), gradient.reshape(ROWS, BY), control.reshape(KLOC, ROWS, BY),
    )
    return out.reshape(KLOC, LEV, BX, BY)


def solution(mesh):
    placed = (
        P("mem", None, "gx", "gy"),
        P(None, "gx", "gy"),
        P("mem", None, "gx", "gy"),
        P(),
        P(),
        P(),
    )
    return jax.shard_map(
        per_device,
        mesh=mesh,
        in_specs=placed,
        out_specs=P("mem", None, "gx", "gy"),
        check_vma=False,
    )
```

```python
import functools

import jax
import jax.numpy as jnp
from jax import lax
from jax.experimental import pallas as pl
from jax.experimental.pallas import tpu as pltpu
from jax.sharding import PartitionSpec as P

MESH = pl.DeviceIdType.MESH
F32 = jnp.float32
BF16 = jnp.bfloat16

LEV, MEMBERS, NX, NY = 64, 8, 256, 1024
MEM, GX, GY = 4, 16, 8
KLOC = MEMBERS // MEM
BX, BY = NX // GX, NY // GY
ROWS = LEV * BX
GROUPS = LEV // 4
QUARTER = ROWS // MEM
CHUNKS = 4
CHUNK = LEV // CHUNKS

NT = (((1,), (1,)), ((), ()))
NN = (((1,), (0,)), ((), ()))
TN = (((0,), (0,)), ((), ()))


def dot(a, b, dims):
    return lax.dot_general(a, b, dims, preferred_element_type=F32)


def split(x):
    hi = x.astype(BF16)
    return hi, (x - hi.astype(F32)).astype(BF16)


def iota(shape, axis):
    return lax.broadcasted_iota(jnp.int32, shape, axis)


def log_decay(r):
    return -r * (1.0 + r * (0.5 + r * (1.0 / 3 + r * (0.25 + r * (0.2 + r * (1.0 / 6))))))


class Line:
    def __init__(self, rate, total, size, index):
        r = rate
        self.rate = r
        self.log = log_decay(r)
        self.a = 1.0 - r
        self.g = self.a * self.a / (r * (1.0 + self.a))
        self.s = (index * size).astype(F32)
        self.last = self.s + (size - 1.0)
        self.n2 = 2.0 * total - self.last
        self.p_s = self.power(self.s)
        self.p_inv = self.power(-self.last)
        self.p_n2 = self.power(self.n2)
        self.ga = self.g * self.power(2.0 * total)
        self.G = 1.0 + 2.0 * self.g + self.ga
        self.total = total
        self.e = self.s + size

    def reach(self, t):
        near = t + self.g + self.ga - self.g * self.power(2.0 * (self.total - t))
        far = self.g * (self.power(-t - 1.0) - self.power(t - 1.0))
        return near, far

    def power(self, m):
        return jnp.exp(self.log * m)

    def sums(self, r1, r2, q1, q2):
        sa = self.p_inv * r1
        fq = self.p_s * q1
        sb = self.p_inv * (self.last * r1 - r2) + self.g * fq
        lh = fq - self.p_n2 * r1
        la = self.p_s * ((self.s + self.G) * q1 + q2) - self.p_n2 * ((self.n2 + self.G) * r1 + r2)
        return sa, sb, la, lh


def kernel(rates_h, bands_h, weights_h, members, gradient, out,
           rates, bands, weights, mem_v, grad_v, psum, total, rs_rcv, vbuf, zbuf, wtab, lsub, thi, tlo,
           mu, ysum, yone, xsum, xrs, xmn, ysnd, yrcv, zsnd, zrcv, kap, xst, xpair, xin, xout, xss, xsr,
           cown, csib, ctot, crcv, xr, xf, fbuf,
           in_sem, rs_s, rs_r, ag_s, ag_r, o_s, o_r, xs_s, xs_r, xa_s, xa_r, y_s, y_r, h_s, h_r, p_s, p_r,
           c_s, c_r, d_s, d_r, k_s, k_r, l_s, l_r):
    i = lax.axis_index("mem")
    gx = lax.axis_index("gx")
    gy = lax.axis_index("gy")
    z, core = gx // 2, gx % 2
    yy, hh = gy // 2, gy % 2

    barrier = pltpu.get_barrier_semaphore()

    def signal(dev):
        pl.semaphore_signal(barrier, inc=1, device_id=dev, device_id_type=MESH)

    sibling = (i, gx + 1 - 2 * core, gy)
    across = (i, gx, gy + 1 - 2 * hh)
    peers = [((i + d) % MEM, gx, gy) for d in range(1, MEM)]
    y_at = [(yy + d) % 4 for d in range(1, 4)]
    chips = [(i, ((z + d) % 8) * 2 + core, gy) for d in range(1, 8)]
    signal(across)
    for dev in chips[2:5] + chips[1:2] + chips[5:6] + chips[0:1] + chips[6:7]:
        signal(dev)
    for d in range(3):
        signal(peers[d])
        signal((i, gx, y_at[d] * 2 + hh))
    signal(sibling)

    loads = [
        pltpu.make_async_copy(rates_h, rates, in_sem.at[0]),
        pltpu.make_async_copy(members, mem_v, in_sem.at[1]),
        pltpu.make_async_copy(gradient, grad_v, in_sem.at[2]),
        pltpu.make_async_copy(weights_h, weights, in_sem.at[3]),
        pltpu.make_async_copy(bands_h, bands, in_sem.at[4]),
    ]
    for load in loads:
        load.start()

    def remote(src, dst, ss, rs, dev):
        return pltpu.make_async_remote_copy(
            src_ref=src, dst_ref=dst, send_sem=ss, recv_sem=rs, device_id=dev, device_id_type=MESH)

    loads[0].wait()
    sub8 = iota((8, 128), 0)
    for t in range(LEV // 8):
        v = jnp.zeros((8, 128), F32)
        for j in range(8):
            v = jnp.where(sub8 == j, rates[t * 8 + j], v)
        lsub[t * 8:(t + 1) * 8, :] = v
    lane = iota((GROUPS, 128), 1)
    lev_id = iota((GROUPS, 128), 0) * 4 + (lane // BX) % 4
    rate_lane = jnp.zeros((GROUPS, 128), F32)
    for l in range(LEV):
        rate_lane = jnp.where(lev_id == l, rates[l], rate_lane)
    ly = Line(rate_lane, NY, BY, gy)
    lx = Line(lsub[...], NX, BX, gx)
    a_sub = lx.a

    cell = iota((8, 128), 1).astype(F32)
    kind = sub8 % 4
    dist = jnp.where(kind < 2, 127.0 - cell, cell)
    factor = jnp.where(kind % 2 == 0, 1.0, dist)

    def basis(l, carry):
        lg = log_decay(jnp.broadcast_to(lsub[pl.ds(l, 1), :], (8, 128)))
        wtab[pl.ds(pl.multiple_of(l * 8, 8), 8), :] = jnp.exp(dist * lg) * factor
        return carry

    lax.fori_loop(0, LEV, basis, 0, unroll=8)

    loads[1].wait()
    loads[2].wait()
    lane8 = (iota((8, 128), 1) // BX) % 4

    def product(g, carry):
        at = pl.multiple_of(g * 64, 64)
        gr = grad_v[pl.ds(at, 64), :]
        m0 = mem_v[0, pl.ds(at, 64), :].astype(F32)
        m1 = mem_v[1, pl.ds(at, 64), :].astype(F32)
        psum[pl.ds(at, 64), :] = m0 + m1
        v0 = m0 * gr
        v1 = m1 * gr
        vbuf[0, pl.ds(at, 64), :] = v0
        vbuf[1, pl.ds(at, 64), :] = v1
        vh, vl = split(jnp.concatenate([v0, v1], axis=0))
        wh, wl = split(wtab[pl.ds(pl.multiple_of(g * 32, 32), 32), :])
        res = dot(wh, vh, NT) + dot(wh, vl, NT) + dot(wl, vh, NT)
        m8 = jnp.zeros((8, 128), F32)
        for lv in range(4):
            m8 = jnp.where(lane8 == lv, res[lv * 8:lv * 8 + 8, :], m8)
        mu[pl.ds(pl.multiple_of(g * 8, 8), 8), :] = m8
        return carry

    lax.fori_loop(0, GROUPS, product, 0, unroll=GROUPS)
    ymom = [mu[pl.ds(q, GROUPS, stride=8), :] for q in range(4)]
    low = lane < 64
    two = [m + pltpu.roll(m, 64, 1) for m in ymom]
    ysum[0] = jnp.where(low, two[0], two[1])
    ysum[1] = jnp.where(low, two[2], two[3])

    pl.semaphore_wait(barrier, 15)
    one = [remote(ysum, yone.at[d], o_s.at[d], o_r.at[d], peers[d]) for d in range(3)]
    for cp in one:
        cp.start()

    for k in range(KLOC):
        r1 = jnp.zeros((LEV, 128), F32)
        r2, q1, q2 = r1, r1, r1
        for x in range(BX):
            v = vbuf[k, pl.ds(x, LEV, stride=BX), :]
            t = a_sub * r1
            r2 = a_sub * r2 + t
            r1 = t + v
            v = vbuf[k, pl.ds(BX - 1 - x, LEV, stride=BX), :]
            t = a_sub * q1
            q2 = a_sub * q2 + t
            q1 = t + v
        for q, s in enumerate(lx.sums(r1, r2, q1, q2)):
            xst[k, q] = s
            if k == 1:
                xsum[q] = xst[0, q] + s
    own16 = pl.multiple_of(i * 16, 16)
    xrc = [remote(xsum.at[:, pl.ds(pl.multiple_of(peers[d][0] * 16, 16), 16)], xrs.at[d],
                  xs_s.at[d], xs_r.at[d], peers[d]) for d in range(3)]
    for cp in xrc:
        cp.start()
    rs = [remote(psum.at[pl.ds(pl.multiple_of(peers[d][0] * QUARTER, QUARTER), QUARTER)], rs_rcv.at[d],
                 rs_s.at[d], rs_r.at[d], peers[d]) for d in range(3)]
    for cp in rs:
        cp.start()

    di = jnp.abs(iota((BY, BY), 0) - iota((BY, BY), 1)).astype(F32)

    def toeplitz(l, carry):
        r = jnp.broadcast_to(lsub[pl.ds(l, 1), :], (8, 128))
        lg = log_decay(r)
        a = 1.0 - r
        c = 1.0 + 2.0 * (a * a / (r * (1.0 + a)))
        lg = jnp.broadcast_to(lg[0:1, :], (BY, BY))
        c = jnp.broadcast_to(c[0:1, :], (BY, BY))
        hi, lo = split(jnp.exp(di * lg) * (di + c))
        at = pl.multiple_of(l * BY, BY)
        thi[pl.ds(at, BY), :] = hi
        tlo[pl.ds(at, BY), :] = lo
        return carry

    lax.fori_loop(0, LEV, toeplitz, 0, unroll=2)

    for cp in one:
        cp.wait()
    tot = [ysum[j] + yone[0, j] + yone[1, j] + yone[2, j] for j in range(2)]
    swap = [pltpu.roll(t, 64, 1) for t in tot]
    mean = [jnp.where(low, tot[0], swap[0]), jnp.where(low, swap[0], tot[0]),
            jnp.where(low, tot[1], swap[1]), jnp.where(low, swap[1], tot[1])]
    r1, r2, q1, q2 = [m - t * (1.0 / MEMBERS) for m, t in zip(ymom, mean)]
    own_y = ly.sums(r1, r2, q1, q2)
    for q in range(4):
        ysnd[q] = own_y[q]
    ycp = []
    for d in range(3):
        part = pl.multiple_of(jnp.where(y_at[d] > yy, 0, 2), 2)
        cp = remote(ysnd.at[pl.ds(part, 2)], yrcv.at[d], y_s.at[d], y_r.at[d], (i, gx, y_at[d] * 2 + hh))
        cp.start()
        ycp.append(cp)

    for cp in xrc:
        cp.wait()
    xmn[:, pl.ds(own16, 16)] = (xsum[:, pl.ds(own16, 16)] + xrs[0] + xrs[1] + xrs[2]) * (1.0 / MEMBERS)
    xag = [remote(xmn.at[:, pl.ds(own16, 16)], xmn.at[:, pl.ds(own16, 16)], xa_s.at[d], xa_r.at[d], peers[d])
           for d in range(3)]
    for cp in xag:
        cp.start()

    for cp in ycp:
        cp.wait()
    zero = jnp.zeros((GROUPS, 128), F32)
    sa = sb = la = lh = zero
    for d in range(3):
        from_left = (yy - (d + 1)) >= 0
        u, w = yrcv[d, 0], yrcv[d, 1]
        sa = sa + jnp.where(from_left, u, 0.0)
        sb = sb + jnp.where(from_left, w, 0.0)
        la = la + jnp.where(from_left, 0.0, u)
        lh = lh + jnp.where(from_left, 0.0, w)
    zsnd[0] = sa + jnp.where(hh == 0, own_y[0], 0.0)
    zsnd[1] = sb + jnp.where(hh == 0, own_y[1], 0.0)
    zsnd[2] = la + jnp.where(hh == 1, own_y[2], 0.0)
    zsnd[3] = lh + jnp.where(hh == 1, own_y[3], 0.0)
    hcp = remote(zsnd, zrcv, h_s, h_r, across)
    hcp.start()

    for cp in xag:
        cp.wait()
    for k in range(KLOC):
        xst[k] = xst[k] - xmn[...]
    pcp = remote(xst.at[1 - core], xpair, p_s, p_r, sibling)
    pcp.start()

    pcp.wait()

    def chain(turn):
        way = ((z >= 4).astype(jnp.int32) + turn) % 2
        has_in = jnp.where(way == 0, z > 0, z < 7)
        has_out = jnp.where(way == 0, z < 7, z > 0)
        target = (i, gx + 2 - 4 * way, gy)
        part = pl.multiple_of(way * 2, 2)

        def copy(c):
            rows = pl.ds(c * CHUNK, CHUNK)
            return remote(xout.at[way, :, rows], xin.at[way, :, rows], c_s.at[way, c], c_r.at[way, c], target)

        @pl.when(jnp.logical_not(has_in))
        def _():
            xin[way] = jnp.zeros((2, LEV, 128), F32)

        for c in range(CHUNKS):
            rows = slice(c * CHUNK, (c + 1) * CHUNK)

            @pl.when(has_in)
            def _():
                copy(c).wait_recv()

            @pl.when(has_out)
            def _():
                xout[way, :, rows] = (xin[way, :, rows] + xst[core, pl.ds(part, 2), rows]
                                      + xpair[pl.ds(part, 2), rows])
                copy(c).start()

        add = jnp.where(way == core, 1.0, 0.0)
        xss[way] = xin[way] + add * xst[core, pl.ds(part, 2)]
        sib = remote(xss.at[way], xsr.at[way], d_s.at[way], d_r.at[way], sibling)
        sib.start()
        xin[way] = xin[way] + (1.0 - add) * xpair[pl.ds(part, 2)]
        return way, has_out, copy, sib

    def drain(done):
        for way, has_out, copy, sib in done:
            sib.wait()
            for c in range(CHUNKS):
                @pl.when(has_out)
                def _():
                    copy(c).wait_send()

    done = [chain(0)]
    own = pl.multiple_of(i * QUARTER, QUARTER)
    for cp in rs:
        cp.wait()
    total[pl.ds(own, QUARTER), :] = (psum[pl.ds(own, QUARTER), :] + rs_rcv[0]
                                     + rs_rcv[1] + rs_rcv[2])
    ag = [remote(total.at[pl.ds(own, QUARTER)], total.at[pl.ds(own, QUARTER)], ag_s.at[d], ag_r.at[d], peers[d])
          for d in range(3)]
    for cp in ag:
        cp.start()

    hcp.wait()
    sa = sa + zrcv[0]
    sb = sb + zrcv[1]
    la = la + zrcv[2]
    lh = lh + zrcv[3]
    k1 = (ly.p_n2 * (sb - sa * (ly.n2 + ly.G)) + ly.p_inv * (la - lh * ly.last)
          + ly.ga * ly.p_inv * (ly.p_s * q1)
          - ly.p_n2 * ly.p_inv * ((2.0 * (NY - ly.last) + ly.G) * r1 + r2))
    k2 = lh * ly.p_inv - sa * ly.p_n2 - ly.p_n2 * ly.p_inv * r1
    k3 = ly.p_s * (sa * (ly.s + ly.G) - sb - lh * ly.g + ly.ga * ly.p_inv * r1 - ly.g * ly.p_s * q1)
    k4 = sa * ly.p_s
    kk = (k1, k2, k3, k4)

    lxl = Line(rate_lane, NX, BX, gx)
    xc = (lane % BX).astype(F32)
    up, down = lxl.power(xc), lxl.power(BX - 1.0 - xc)
    wts = lxl.sums(down, (BX - 1.0 - xc) * down, up, xc * up)
    stack = jnp.concatenate([w * kq for w in wts for kq in kk], axis=0)
    seg = (iota((128, 128), 0) // BX == iota((128, 128), 1) // BX).astype(BF16)
    sh, sl = split(stack)
    res = dot(sh, seg, NN) + dot(sl, seg, NN)
    slot = lane % BX
    cor = zero
    for c in range(16):
        cor = jnp.where(slot == c, res[c * GROUPS:(c + 1) * GROUPS], cor)
    cown[...] = cor
    lcp = remote(cown, csib, l_s, l_r, sibling)
    lcp.start()
    for q, k in enumerate(kk + (zero,) * 4):
        kap[pl.ds(q, GROUPS, stride=8), :] = k

    def spread():
        lcp.wait()
        ctot[...] = cor + csib[...]
        for d in (3, 2, 4, 1, 5, 0, 6):
            ccp[d].start()

    ccp = [remote(ctot, crcv.at[d], k_s.at[d], k_r.at[d], chips[d]) for d in range(7)]

    def local_y(l, carry):
        at = pl.multiple_of(l * BX, BX)
        tt = pl.multiple_of(l * BY, BY)
        mean = total[pl.ds(at, BX), :] * (1.0 / MEMBERS)
        gr = grad_v[pl.ds(at, BX), :]
        v = jnp.concatenate([(mem_v[k, pl.ds(at, BX), :].astype(F32) - mean) * gr for k in range(KLOC)], axis=0)
        n = KLOC * BX
        both = jnp.concatenate([thi[pl.ds(tt, BY), :], tlo[pl.ds(tt, BY), :]], axis=1)
        res = dot(jnp.concatenate(split(v), axis=0), both, NN)
        res = res[:n, :BY] + res[n:, :BY] + res[:n, BY:]
        zbuf[0, pl.ds(at, BX), :] = res[0:BX]
        zbuf[1, pl.ds(at, BX), :] = res[BX:]
        return carry

    def synth(g, carry):
        at = pl.multiple_of(g * 64, 64)
        k8 = kap[pl.ds(pl.multiple_of(g * 8, 8), 8), :]
        big = jnp.concatenate([jnp.where(lane8 == lv, k8, 0.0) for lv in range(4)], axis=0)
        kh, kl = split(big)
        wh, wl = split(wtab[pl.ds(pl.multiple_of(g * 32, 32), 32), :])
        res = dot(jnp.concatenate([kh, kl, kh], axis=0), jnp.concatenate([wh, wh, wl], axis=0), TN)
        zbuf[0, pl.ds(at, 64), :] += res[0:64]
        zbuf[1, pl.ds(at, 64), :] += res[64:]
        return carry

    def block():
        for cp in ag:
            cp.wait()
        lax.fori_loop(0, LEV, local_y, 0, unroll=8)
        lax.fori_loop(0, GROUPS, synth, 0, unroll=4)

    middle = (z >= 2) & (z <= 5)
    centre = (z == 3) | (z == 4)

    @pl.when(jnp.logical_not(centre))
    def _():
        spread()

    for load in loads[3:5]:
        load.wait()
    alpha = lx.rate / (1.0 + a_sub)
    scale = 2.0 * lx.rate * lx.rate * lx.rate * alpha * alpha
    pid = iota((LEV, LEV), 0)
    lid = iota((LEV, LEV), 1)
    keep = jnp.abs(pid - lid) <= bands[...]
    mixed = jnp.where(keep, weights[...], 0.0) * scale[:, 0:LEV]
    mh, ml = split(mixed.T)
    mcat = jnp.concatenate([mh, mh, ml], axis=1)

    def rest():
        block()

    @pl.when(jnp.logical_not(middle))
    def _():
        rest()

    done.append(chain(1))

    @pl.when(centre)
    def _():
        spread()

    @pl.when(middle)
    def _():
        rest()

    drain(done)

    for k in range(KLOC):
        for q in range(4):
            row = (k * 4 + q) * LEV
            xr[row:row + LEV, :] = jnp.where(core == k, xin[q // 2, q % 2], xsr[q // 2, q % 2])

    def local_x(l, carry):
        tt = pl.multiple_of(l * BY, BY)
        vh, vl = split(xr[pl.ds(l, 8, stride=LEV), :])
        th = thi[pl.ds(tt, BY), :]
        xf[pl.ds(l, 8, stride=LEV), :] = dot(jnp.concatenate([vh, vl, vh], axis=1),
                                             jnp.concatenate([th, th, tlo[pl.ds(tt, BY), :]], axis=0), NN)
        return carry

    lax.fori_loop(0, LEV, local_x, 0, unroll=16)
    for cp in ccp:
        cp.wait()
    right = slot < 8
    cst = jnp.where(right == (core == 1), csib[...], 0.0)
    for d in range(7):
        from_left = (z - (d + 1)) >= 0
        cst = cst + jnp.where(right == from_left, crcv[d], 0.0)
    cown[...] = cst
    zr, zc = iota((64, 256), 0), iota((64, 256), 1)
    fits = ((zr // 32 == (zc // 64) % 2) & ((zr // 8) % 4 == (zc // 4) % 4)
            & ((zr % 8) // 4 == zc // 128) & (zr % 4 == (zc // 16) % 4))

    def synth_x(t, carry):
        row = jnp.concatenate([cown[pl.ds(2 * t, 1), :], cown[pl.ds(2 * t + 1, 1), :]], axis=1)
        kh, kl = split(jnp.where(fits, jnp.broadcast_to(row, (64, 256)), 0.0))
        w = wtab[pl.ds(pl.multiple_of(t * 64, 64), 64), :]
        tiles = [w[(g * 4 + lv) * 8:(g * 4 + lv) * 8 + 8] for g in range(2) for k in range(2)
                 for lv in range(4) for twice in range(2)]
        wh, wl = split(jnp.concatenate(tiles, axis=0))
        res = dot(kh, wh, NN) + dot(kl, wh, NN) + dot(kh, wl, NN)
        for j in range(8):
            xf[pl.ds(pl.multiple_of(j * LEV + t * 8, 8), 8), :] += res[j * 8:(j + 1) * 8]
        return carry

    lax.fori_loop(0, LEV // 8, synth_x, 0, unroll=8)

    g, s, e, G = lx.g, lx.s, lx.e, lx.G
    ge = 1.0 + g
    p_s, p_e, p_me, p_2e = lx.power(s), lx.power(e), lx.power(-e), lx.power(2.0 * NX - e)
    hx = p_e - p_2e
    ux = p_e * (e + G) - p_2e * (2.0 * NX - e + G)
    hs = p_s - lx.power(2.0 * NX - s)
    p_s1, p_1e = lx.power(s - 1.0), lx.power(1.0 - e)
    near_s, far_s = lx.reach(s)
    near_e, far_e = lx.reach(e)

    for k in range(KLOC):
        for t in range(LEV // 8):
            lo = t * 8
            cut = lambda m: m[lo:lo + 8]
            sa, sb, la, lh = [xf[(k * 4 + q) * LEV + lo:(k * 4 + q) * LEV + lo + 8, :] for q in range(4)]
            a8, ge8, hx8, pm8 = cut(a_sub), cut(ge), cut(hx), cut(p_me)
            line = [zbuf[k, pl.ds(lo * BX + x, 8, stride=BX), :] for x in range(BX)]

            def sweep(run, order):
                for x in range(BX)[::order]:
                    run = a8 * run + line[x]
                    line[x] = run
                return run

            sa_e = cut(p_1e) * sweep(cut(p_s1) * sa, 1)
            first = sweep(ge8 * (hx8 * sa_e + pm8 * lh), -1)
            lh_s = cut(p_s) * (first / ge8 - cut(hs) * sa)
            last = sweep(ge8 * (cut(p_s1) * (cut(near_s) * sa - sb) + cut(far_s) * lh_s), 1)
            sb_e = cut(near_e) * sa_e - cut(p_1e) * (last / ge8 - cut(far_e) * lh)
            sweep(ge8 * ge8 * (cut(ux) * sa_e - hx8 * sb_e + pm8 * la - (e * pm8 + cut(g) * cut(p_e)) * lh), -1)
            for x in range(BX):
                fbuf[k, x, lo:lo + 8, :] = line[x]

    def mix(x, carry):
        for k in range(KLOC):
            fh, fl = split(fbuf[k, x])
            fcat = jnp.concatenate([fh, fl, fh], axis=0)
            out[k, pl.ds(x, LEV, stride=BX), :] = dot(mcat, fcat, NN)
        return carry

    lax.fori_loop(0, BX, mix, 0, unroll=8)


def per_device(members, gradient, control, filter_rates, vertical_weights, band_widths):
    hbm = pl.BlockSpec(memory_space=pltpu.HBM)
    dma = pltpu.SemaphoreType.DMA

    def vm(*shape):
        return pltpu.VMEM(shape, F32)

    three = [dma((3,))] * 2
    single = [dma] * 2
    out = pl.pallas_call(
        kernel,
        out_shape=jax.ShapeDtypeStruct((KLOC, ROWS, BY), F32),
        in_specs=[hbm] * 5,
        out_specs=pl.BlockSpec(memory_space=pltpu.VMEM),
        scratch_shapes=[
            pltpu.SMEM((LEV,), F32),
            pltpu.VMEM((1, LEV), jnp.int32),
            vm(LEV, LEV),
            pltpu.VMEM((KLOC, ROWS, BY), BF16),
            vm(ROWS, BY),
            vm(ROWS, BY), vm(ROWS, BY), vm(3, QUARTER, BY),
            vm(KLOC, ROWS, BY), vm(KLOC, ROWS, BY),
            vm(LEV * 8, 128), vm(LEV, 128),
            pltpu.VMEM((LEV * BY, BY), BF16),
            pltpu.VMEM((LEV * BY, BY), BF16),
            vm(GROUPS * 8, 128),
            vm(2, GROUPS, 128), vm(3, 2, GROUPS, 128),
            vm(4, LEV, 128), vm(3, 4, 16, 128), vm(4, LEV, 128),
            vm(4, GROUPS, 128), vm(3, 2, GROUPS, 128), vm(4, GROUPS, 128), vm(4, GROUPS, 128),
            vm(GROUPS * 8, 128),
            vm(KLOC, 4, LEV, 128), vm(4, LEV, 128),
            vm(2, 2, LEV, 128), vm(2, 2, LEV, 128), vm(2, 2, LEV, 128), vm(2, 2, LEV, 128),
            vm(GROUPS, 128), vm(GROUPS, 128), vm(GROUPS, 128), vm(7, GROUPS, 128),
            vm(8 * LEV, 128), vm(8 * LEV, 128),
            vm(KLOC, BX, LEV, BY),
            dma((5,)),
            *three, *three, *three, *three, *three, *three,
            *single, *single,
            dma((2, CHUNKS)), dma((2, CHUNKS)), dma((2,)), dma((2,)),
            dma((7,)), dma((7,)), *single,
        ],
        compiler_params=pltpu.CompilerParams(
            collective_id=0, has_side_effects=True, vmem_limit_bytes=60 << 20),
        name="localize",
    )(
        filter_rates, band_widths.reshape(1, LEV), vertical_weights,
        members.reshape(KLOC, ROWS, BY), gradient.reshape(ROWS, BY),
    )
    return out.reshape(KLOC, LEV, BX, BY) + control.astype(F32)


def solution(mesh):
    placed = (
        P("mem", None, "gx", "gy"),
        P(None, "gx", "gy"),
        P("mem", None, "gx", "gy"),
        P(),
        P(),
        P(),
    )
    return jax.shard_map(
        per_device,
        mesh=mesh,
        in_specs=placed,
        out_specs=P("mem", None, "gx", "gy"),
        check_vma=False,
    )
```

```python
import functools

import jax
import jax.numpy as jnp
from jax import lax
from jax.experimental import pallas as pl
from jax.experimental.pallas import tpu as pltpu
from jax.sharding import PartitionSpec as P

MESH = pl.DeviceIdType.MESH
F32 = jnp.float32
BF16 = jnp.bfloat16

LEV, MEMBERS, NX, NY = 64, 8, 256, 1024
MEM, GX, GY = 4, 16, 8
KLOC = MEMBERS // MEM
BX, BY = NX // GX, NY // GY
ROWS = LEV * BX
GROUPS = LEV // 4
QUARTER = ROWS // MEM
CHUNKS = 4
CHUNK = LEV // CHUNKS
PARTS = 2
PART = LEV // PARTS

NT = (((1,), (1,)), ((), ()))
NN = (((1,), (0,)), ((), ()))
TN = (((0,), (0,)), ((), ()))


def dot(a, b, dims):
    return lax.dot_general(a, b, dims, preferred_element_type=F32)


def split(x):
    hi = x.astype(BF16)
    return hi, (x - hi.astype(F32)).astype(BF16)


def iota(shape, axis):
    return lax.broadcasted_iota(jnp.int32, shape, axis)


def log_decay(r):
    return -r * (1.0 + r * (0.5 + r * (1.0 / 3 + r * (0.25 + r * (0.2 + r * (1.0 / 6))))))


class Line:
    def __init__(self, rate, total, size, index):
        r = rate
        self.rate = r
        self.log = log_decay(r)
        self.a = 1.0 - r
        self.g = self.a * self.a / (r * (1.0 + self.a))
        self.s = (index * size).astype(F32)
        self.last = self.s + (size - 1.0)
        self.n2 = 2.0 * total - self.last
        self.p_s = self.power(self.s)
        self.p_inv = self.power(-self.last)
        self.p_n2 = self.power(self.n2)
        self.ga = self.g * self.power(2.0 * total)
        self.G = 1.0 + 2.0 * self.g + self.ga
        self.total = total
        self.e = self.s + size

    def reach(self, t):
        near = t + self.g + self.ga - self.g * self.power(2.0 * (self.total - t))
        far = self.g * (self.power(-t - 1.0) - self.power(t - 1.0))
        return near, far

    def power(self, m):
        return jnp.exp(self.log * m)

    def sums(self, r1, r2, q1, q2):
        sa = self.p_inv * r1
        fq = self.p_s * q1
        sb = self.p_inv * (self.last * r1 - r2) + self.g * fq
        lh = fq - self.p_n2 * r1
        la = self.p_s * ((self.s + self.G) * q1 + q2) - self.p_n2 * ((self.n2 + self.G) * r1 + r2)
        return sa, sb, la, lh


def kernel(rates_h, bands_h, weights_h, members, gradient, out,
           rates, bands, weights, mem_v, grad_v, psum, total, rs_rcv, vbuf, zbuf, wtab, lsub, thi, tlo,
           mu, ysum, yone, xsum, xrs, xmn, xrt, ysnd, yrcv, zsnd, zrcv, kap, xst, xpair, xin, xout, xss, xsr,
           cown, csib, ctot, crcv, xr, xf, fbuf,
           in_sem, rs_s, rs_r, ag_s, ag_r, o_s, o_r, xs_s, xs_r, y_s, y_r, h_s, h_r, p_s, p_r,
           c_s, c_r, d_s, d_r, k_s, k_r, l_s, l_r):
    i = lax.axis_index("mem")
    gx = lax.axis_index("gx")
    gy = lax.axis_index("gy")
    z, core = gx // 2, gx % 2
    yy, hh = gy // 2, gy % 2

    barrier = pltpu.get_barrier_semaphore()

    def signal(dev):
        pl.semaphore_signal(barrier, inc=1, device_id=dev, device_id_type=MESH)

    sibling = (i, gx + 1 - 2 * core, gy)
    across = (i, gx, gy + 1 - 2 * hh)
    peers = [((i + d) % MEM, gx, gy) for d in range(1, MEM)]
    y_at = [(yy + d) % 4 for d in range(1, 4)]
    chips = [(i, ((z + d) % 8) * 2 + core, gy) for d in range(1, 8)]
    signal(across)
    for dev in chips[2:5] + chips[1:2] + chips[5:6] + chips[0:1] + chips[6:7]:
        signal(dev)
    for d in range(3):
        signal(peers[d])
        signal((i, gx, y_at[d] * 2 + hh))
    signal(sibling)

    loads = [
        pltpu.make_async_copy(rates_h, rates, in_sem.at[0]),
        pltpu.make_async_copy(members, mem_v, in_sem.at[1]),
        pltpu.make_async_copy(gradient, grad_v, in_sem.at[2]),
        pltpu.make_async_copy(weights_h, weights, in_sem.at[3]),
        pltpu.make_async_copy(bands_h, bands, in_sem.at[4]),
    ]
    for load in loads:
        load.start()

    def remote(src, dst, ss, rs, dev):
        return pltpu.make_async_remote_copy(
            src_ref=src, dst_ref=dst, send_sem=ss, recv_sem=rs, device_id=dev, device_id_type=MESH)

    loads[0].wait()
    sub8 = iota((8, 128), 0)
    for t in range(LEV // 8):
        v = jnp.zeros((8, 128), F32)
        for j in range(8):
            v = jnp.where(sub8 == j, rates[t * 8 + j], v)
        lsub[t * 8:(t + 1) * 8, :] = v
    lane = iota((GROUPS, 128), 1)
    lev_id = iota((GROUPS, 128), 0) * 4 + (lane // BX) % 4
    rate_lane = jnp.zeros((GROUPS, 128), F32)
    for l in range(LEV):
        rate_lane = jnp.where(lev_id == l, rates[l], rate_lane)
    ly = Line(rate_lane, NY, BY, gy)
    lx = Line(lsub[...], NX, BX, gx)
    a_sub = lx.a

    cell = iota((8, 128), 1).astype(F32)
    kind = sub8 % 4
    dist = jnp.where(kind < 2, 127.0 - cell, cell)
    factor = jnp.where(kind % 2 == 0, 1.0, dist)

    def basis(l, carry):
        lg = log_decay(jnp.broadcast_to(lsub[pl.ds(l, 1), :], (8, 128)))
        wtab[pl.ds(pl.multiple_of(l * 8, 8), 8), :] = jnp.exp(dist * lg) * factor
        return carry

    lax.fori_loop(0, LEV, basis, 0, unroll=8)

    loads[1].wait()
    loads[2].wait()
    lane8 = (iota((8, 128), 1) // BX) % 4

    def product(g, carry):
        at = pl.multiple_of(g * 64, 64)
        gr = grad_v[pl.ds(at, 64), :]
        m0 = mem_v[0, pl.ds(at, 64), :].astype(F32)
        m1 = mem_v[1, pl.ds(at, 64), :].astype(F32)
        psum[pl.ds(at, 64), :] = m0 + m1
        v0 = m0 * gr
        v1 = m1 * gr
        vbuf[0, pl.ds(at, 64), :] = v0
        vbuf[1, pl.ds(at, 64), :] = v1
        vh, vl = split(jnp.concatenate([v0, v1], axis=0))
        wh, wl = split(wtab[pl.ds(pl.multiple_of(g * 32, 32), 32), :])
        res = dot(wh, vh, NT) + dot(wh, vl, NT) + dot(wl, vh, NT)
        m8 = jnp.zeros((8, 128), F32)
        for lv in range(4):
            m8 = jnp.where(lane8 == lv, res[lv * 8:lv * 8 + 8, :], m8)
        mu[pl.ds(pl.multiple_of(g * 8, 8), 8), :] = m8
        return carry

    lax.fori_loop(0, GROUPS, product, 0, unroll=GROUPS)
    ymom = [mu[pl.ds(q, GROUPS, stride=8), :] for q in range(4)]
    low = lane < 64
    two = [m + pltpu.roll(m, 64, 1) for m in ymom]
    ysum[0] = jnp.where(low, two[0], two[1])
    ysum[1] = jnp.where(low, two[2], two[3])

    pl.semaphore_wait(barrier, 15)
    one = [remote(ysum, yone.at[d], o_s.at[d], o_r.at[d], peers[d]) for d in range(3)]
    for cp in one:
        cp.start()

    for k in range(KLOC):
        r1 = jnp.zeros((LEV, 128), F32)
        r2, q1, q2 = r1, r1, r1
        for x in range(BX):
            v = vbuf[k, pl.ds(x, LEV, stride=BX), :]
            t = a_sub * r1
            r2 = a_sub * r2 + t
            r1 = t + v
            v = vbuf[k, pl.ds(BX - 1 - x, LEV, stride=BX), :]
            t = a_sub * q1
            q2 = a_sub * q2 + t
            q1 = t + v
        for q, s in enumerate(lx.sums(r1, r2, q1, q2)):
            xst[k, q] = s
            if k == 1:
                xsum[q] = xst[0, q] + s
    ring = [(i + 1 - 2 * (i % 2), gx, gy), (3 - i, gx, gy)]

    def piece(ref, half, c):
        return ref.at[2 * half:2 * half + 2, c * PART:(c + 1) * PART]

    def round_of(step, src, dst):
        return [[remote(piece(src, half, c), piece(dst, half, c), xs_s.at[step, half, c], xs_r.at[step, half, c],
                        ring[(half + step) % 2]) for half in range(2)] for c in range(PARTS)]

    near = round_of(0, xsum, xrs)
    far = round_of(1, xmn, xrt)
    for pair in near:
        for cp in pair:
            cp.start()
    di = jnp.abs(iota((BY, BY), 0) - iota((BY, BY), 1)).astype(F32)

    def toeplitz(l, carry):
        r = jnp.broadcast_to(lsub[pl.ds(l, 1), :], (8, 128))
        lg = log_decay(r)
        a = 1.0 - r
        c = 1.0 + 2.0 * (a * a / (r * (1.0 + a)))
        lg = jnp.broadcast_to(lg[0:1, :], (BY, BY))
        c = jnp.broadcast_to(c[0:1, :], (BY, BY))
        hi, lo = split(jnp.exp(di * lg) * (di + c))
        at = pl.multiple_of(l * BY, BY)
        thi[pl.ds(at, BY), :] = hi
        tlo[pl.ds(at, BY), :] = lo
        return carry

    lax.fori_loop(0, LEV, toeplitz, 0, unroll=2)

    for cp in one:
        cp.wait()
    tot = [ysum[j] + yone[0, j] + yone[1, j] + yone[2, j] for j in range(2)]
    swap = [pltpu.roll(t, 64, 1) for t in tot]
    mean = [jnp.where(low, tot[0], swap[0]), jnp.where(low, swap[0], tot[0]),
            jnp.where(low, tot[1], swap[1]), jnp.where(low, swap[1], tot[1])]
    r1, r2, q1, q2 = [m - t * (1.0 / MEMBERS) for m, t in zip(ymom, mean)]
    own_y = ly.sums(r1, r2, q1, q2)
    for q in range(4):
        ysnd[q] = own_y[q]
    ycp = []
    for d in range(3):
        part = pl.multiple_of(jnp.where(y_at[d] > yy, 0, 2), 2)
        cp = remote(ysnd.at[pl.ds(part, 2)], yrcv.at[d], y_s.at[d], y_r.at[d], (i, gx, y_at[d] * 2 + hh))
        cp.start()
        ycp.append(cp)

    for c in range(PARTS):
        rows = slice(c * PART, (c + 1) * PART)
        for cp in near[c]:
            cp.wait()
        xmn[:, rows] = xsum[:, rows] + xrs[:, rows]
        for cp in far[c]:
            cp.start()
    rs = [remote(psum.at[pl.ds(pl.multiple_of(peers[d][0] * QUARTER, QUARTER), QUARTER)], rs_rcv.at[d],
                 rs_s.at[d], rs_r.at[d], peers[d]) for d in range(3)]
    for cp in rs:
        cp.start()

    for cp in ycp:
        cp.wait()
    zero = jnp.zeros((GROUPS, 128), F32)
    sa = sb = la = lh = zero
    for d in range(3):
        from_left = (yy - (d + 1)) >= 0
        u, w = yrcv[d, 0], yrcv[d, 1]
        sa = sa + jnp.where(from_left, u, 0.0)
        sb = sb + jnp.where(from_left, w, 0.0)
        la = la + jnp.where(from_left, 0.0, u)
        lh = lh + jnp.where(from_left, 0.0, w)
    zsnd[0] = sa + jnp.where(hh == 0, own_y[0], 0.0)
    zsnd[1] = sb + jnp.where(hh == 0, own_y[1], 0.0)
    zsnd[2] = la + jnp.where(hh == 1, own_y[2], 0.0)
    zsnd[3] = lh + jnp.where(hh == 1, own_y[3], 0.0)
    hcp = remote(zsnd, zrcv, h_s, h_r, across)
    hcp.start()

    pcp = []
    for c in range(PARTS):
        rows = slice(c * PART, (c + 1) * PART)
        for cp in far[c]:
            cp.wait()
        for q in range(4):
            m = (xmn[q, rows] + xrt[q, rows]) * (1.0 / MEMBERS)
            for k in range(KLOC):
                xst[k, q, rows] = xst[k, q, rows] - m
        cp = remote(xst.at[1 - core, :, rows], xpair.at[:, rows], p_s.at[c], p_r.at[c], sibling)
        cp.start()
        pcp.append(cp)


    def chain(turn):
        way = ((z >= 4).astype(jnp.int32) + turn) % 2
        has_in = jnp.where(way == 0, z > 0, z < 7)
        has_out = jnp.where(way == 0, z < 7, z > 0)
        target = (i, gx + 2 - 4 * way, gy)
        part = pl.multiple_of(way * 2, 2)

        def copy(c):
            rows = pl.ds(c * CHUNK, CHUNK)
            return remote(xout.at[way, :, rows], xin.at[way, :, rows], c_s.at[way, c], c_r.at[way, c], target)

        @pl.when(jnp.logical_not(has_in))
        def _():
            xin[way] = jnp.zeros((2, LEV, 128), F32)

        for c in range(CHUNKS):
            rows = slice(c * CHUNK, (c + 1) * CHUNK)

            if turn == 0 and c % (CHUNKS // PARTS) == 0:
                pcp[c // (CHUNKS // PARTS)].wait()

            @pl.when(has_in)
            def _():
                copy(c).wait_recv()

            @pl.when(has_out)
            def _():
                xout[way, :, rows] = (xin[way, :, rows] + xst[core, pl.ds(part, 2), rows]
                                      + xpair[pl.ds(part, 2), rows])
                copy(c).start()

        add = jnp.where(way == core, 1.0, 0.0)
        xss[way] = xin[way] + add * xst[core, pl.ds(part, 2)]
        sib = remote(xss.at[way], xsr.at[way], d_s.at[way], d_r.at[way], sibling)
        sib.start()
        xin[way] = xin[way] + (1.0 - add) * xpair[pl.ds(part, 2)]
        return way, has_out, copy, sib

    def drain(done):
        for way, has_out, copy, sib in done:
            sib.wait()
            for c in range(CHUNKS):
                @pl.when(has_out)
                def _():
                    copy(c).wait_send()

    done = [chain(0)]
    own = pl.multiple_of(i * QUARTER, QUARTER)
    for cp in rs:
        cp.wait()
    total[pl.ds(own, QUARTER), :] = (psum[pl.ds(own, QUARTER), :] + rs_rcv[0]
                                     + rs_rcv[1] + rs_rcv[2])
    ag = [remote(total.at[pl.ds(own, QUARTER)], total.at[pl.ds(own, QUARTER)], ag_s.at[d], ag_r.at[d], peers[d])
          for d in range(3)]
    for cp in ag:
        cp.start()

    hcp.wait()
    sa = sa + zrcv[0]
    sb = sb + zrcv[1]
    la = la + zrcv[2]
    lh = lh + zrcv[3]
    k1 = (ly.p_n2 * (sb - sa * (ly.n2 + ly.G)) + ly.p_inv * (la - lh * ly.last)
          + ly.ga * ly.p_inv * (ly.p_s * q1)
          - ly.p_n2 * ly.p_inv * ((2.0 * (NY - ly.last) + ly.G) * r1 + r2))
    k2 = lh * ly.p_inv - sa * ly.p_n2 - ly.p_n2 * ly.p_inv * r1
    k3 = ly.p_s * (sa * (ly.s + ly.G) - sb - lh * ly.g + ly.ga * ly.p_inv * r1 - ly.g * ly.p_s * q1)
    k4 = sa * ly.p_s
    kk = (k1, k2, k3, k4)

    lxl = Line(rate_lane, NX, BX, gx)
    xc = (lane % BX).astype(F32)
    up, down = lxl.power(xc), lxl.power(BX - 1.0 - xc)
    wts = lxl.sums(down, (BX - 1.0 - xc) * down, up, xc * up)
    stack = jnp.concatenate([w * kq for w in wts for kq in kk], axis=0)
    seg = (iota((128, 128), 0) // BX == iota((128, 128), 1) // BX).astype(BF16)
    sh, sl = split(stack)
    res = dot(sh, seg, NN) + dot(sl, seg, NN)
    slot = lane % BX
    slot8 = iota((8, 128), 1) % BX < 8
    cor = zero
    for c in range(16):
        cor = jnp.where(slot == c, res[c * GROUPS:(c + 1) * GROUPS], cor)
    cown[...] = cor
    lcp = remote(cown, csib, l_s, l_r, sibling)
    lcp.start()
    for q, k in enumerate(kk + (zero,) * 4):
        kap[pl.ds(q, GROUPS, stride=8), :] = k

    def spread():
        lcp.wait()
        even = cown[pl.ds(0, 8, stride=2), :] + csib[pl.ds(0, 8, stride=2), :]
        odd = cown[pl.ds(1, 8, stride=2), :] + csib[pl.ds(1, 8, stride=2), :]
        ctot[0] = jnp.where(slot8, even, pltpu.roll(odd, 8, 1))
        ctot[1] = jnp.where(slot8, pltpu.roll(even, 120, 1), odd)
        for d in (3, 2, 4, 1, 5, 0, 6):
            ccp[d].start()

    to_right = [(z + d + 1) <= 7 for d in range(7)]
    ccp = [remote(ctot.at[jnp.where(to_right[d], 0, 1)], crcv.at[d], k_s.at[d], k_r.at[d], chips[d]) for d in range(7)]

    def local_y(l, carry):
        at = pl.multiple_of(l * BX, BX)
        tt = pl.multiple_of(l * BY, BY)
        mean = total[pl.ds(at, BX), :] * (1.0 / MEMBERS)
        gr = grad_v[pl.ds(at, BX), :]
        v = jnp.concatenate([(mem_v[k, pl.ds(at, BX), :].astype(F32) - mean) * gr for k in range(KLOC)], axis=0)
        n = KLOC * BX
        both = jnp.concatenate([thi[pl.ds(tt, BY), :], tlo[pl.ds(tt, BY), :]], axis=1)
        res = dot(jnp.concatenate(split(v), axis=0), both, NN)
        res = res[:n, :BY] + res[n:, :BY] + res[:n, BY:]
        zbuf[0, pl.ds(at, BX), :] = res[0:BX]
        zbuf[1, pl.ds(at, BX), :] = res[BX:]
        return carry

    def synth(g, carry):
        at = pl.multiple_of(g * 64, 64)
        k8 = kap[pl.ds(pl.multiple_of(g * 8, 8), 8), :]
        big = jnp.concatenate([jnp.where(lane8 == lv, k8, 0.0) for lv in range(4)], axis=0)
        kh, kl = split(big)
        wh, wl = split(wtab[pl.ds(pl.multiple_of(g * 32, 32), 32), :])
        res = dot(jnp.concatenate([kh, kl, kh], axis=0), jnp.concatenate([wh, wh, wl], axis=0), TN)
        zbuf[0, pl.ds(at, 64), :] += res[0:64]
        zbuf[1, pl.ds(at, 64), :] += res[64:]
        return carry

    def block():
        for cp in ag:
            cp.wait()
        lax.fori_loop(0, LEV, local_y, 0, unroll=8)
        lax.fori_loop(0, GROUPS, synth, 0, unroll=4)

    middle = (z >= 1) & (z <= 6)
    centre = (z == 3) | (z == 4)

    @pl.when(jnp.logical_not(centre))
    def _():
        spread()

    for load in loads[3:5]:
        load.wait()
    alpha = lx.rate / (1.0 + a_sub)
    scale = 2.0 * lx.rate * lx.rate * lx.rate * alpha * alpha
    pid = iota((LEV, LEV), 0)
    lid = iota((LEV, LEV), 1)
    keep = jnp.abs(pid - lid) <= bands[...]
    mixed = jnp.where(keep, weights[...], 0.0) * scale[:, 0:LEV]
    mh, ml = split(mixed.T)
    mcat = jnp.concatenate([mh, mh, ml], axis=1)

    def rest():
        block()

    @pl.when(jnp.logical_not(middle))
    def _():
        rest()

    done.append(chain(1))

    @pl.when(centre)
    def _():
        spread()

    @pl.when(middle)
    def _():
        rest()

    drain(done)

    for k in range(KLOC):
        for q in range(4):
            row = (k * 4 + q) * LEV
            xr[row:row + LEV, :] = jnp.where(core == k, xin[q // 2, q % 2], xsr[q // 2, q % 2])

    def local_x(l, carry):
        tt = pl.multiple_of(l * BY, BY)
        vh, vl = split(xr[pl.ds(l, 8, stride=LEV), :])
        th = thi[pl.ds(tt, BY), :]
        xf[pl.ds(l, 8, stride=LEV), :] = dot(jnp.concatenate([vh, vl, vh], axis=1),
                                             jnp.concatenate([th, th, tlo[pl.ds(tt, BY), :]], axis=0), NN)
        return carry

    lax.fori_loop(0, LEV, local_x, 0, unroll=16)
    for cp in ccp:
        cp.wait()
    to_me, to_us = jnp.zeros((8, 128), F32), jnp.zeros((8, 128), F32)
    for d in range(7):
        from_left = (z - (d + 1)) >= 0
        to_me = to_me + jnp.where(from_left, crcv[d], 0.0)
        to_us = to_us + jnp.where(from_left, 0.0, crcv[d])
    mate = jnp.where((slot < 8) == (core == 1), csib[...], 0.0)
    cown[...] = mate
    cown[pl.ds(0, 8, stride=2), :] += jnp.where(slot8, to_me, pltpu.roll(to_us, 8, 1))
    cown[pl.ds(1, 8, stride=2), :] += jnp.where(slot8, pltpu.roll(to_me, 120, 1), to_us)
    zr, zc = iota((64, 256), 0), iota((64, 256), 1)
    fits = ((zr // 32 == (zc // 64) % 2) & ((zr // 8) % 4 == (zc // 4) % 4)
            & ((zr % 8) // 4 == zc // 128) & (zr % 4 == (zc // 16) % 4))

    def synth_x(t, carry):
        row = jnp.concatenate([cown[pl.ds(2 * t, 1), :], cown[pl.ds(2 * t + 1, 1), :]], axis=1)
        kh, kl = split(jnp.where(fits, jnp.broadcast_to(row, (64, 256)), 0.0))
        w = wtab[pl.ds(pl.multiple_of(t * 64, 64), 64), :]
        tiles = [w[(g * 4 + lv) * 8:(g * 4 + lv) * 8 + 8] for g in range(2) for k in range(2)
                 for lv in range(4) for twice in range(2)]
        wh, wl = split(jnp.concatenate(tiles, axis=0))
        res = dot(kh, wh, NN) + dot(kl, wh, NN) + dot(kh, wl, NN)
        for j in range(8):
            xf[pl.ds(pl.multiple_of(j * LEV + t * 8, 8), 8), :] += res[j * 8:(j + 1) * 8]
        return carry

    lax.fori_loop(0, LEV // 8, synth_x, 0, unroll=8)

    g, s, e, G = lx.g, lx.s, lx.e, lx.G
    ge = 1.0 + g
    p_s, p_e, p_me, p_2e = lx.power(s), lx.power(e), lx.power(-e), lx.power(2.0 * NX - e)
    hx = p_e - p_2e
    ux = p_e * (e + G) - p_2e * (2.0 * NX - e + G)
    hs = p_s - lx.power(2.0 * NX - s)
    p_s1, p_1e = lx.power(s - 1.0), lx.power(1.0 - e)
    near_s, far_s = lx.reach(s)
    near_e, far_e = lx.reach(e)

    for k in range(KLOC):
        for t in range(LEV // 8):
            lo = t * 8
            cut = lambda m: m[lo:lo + 8]
            sa, sb, la, lh = [xf[(k * 4 + q) * LEV + lo:(k * 4 + q) * LEV + lo + 8, :] for q in range(4)]
            a8, ge8, hx8, pm8 = cut(a_sub), cut(ge), cut(hx), cut(p_me)
            line = [zbuf[k, pl.ds(lo * BX + x, 8, stride=BX), :] for x in range(BX)]

            def sweep(run, order):
                for x in range(BX)[::order]:
                    run = a8 * run + line[x]
                    line[x] = run
                return run

            sa_e = cut(p_1e) * sweep(cut(p_s1) * sa, 1)
            first = sweep(ge8 * (hx8 * sa_e + pm8 * lh), -1)
            lh_s = cut(p_s) * (first / ge8 - cut(hs) * sa)
            last = sweep(ge8 * (cut(p_s1) * (cut(near_s) * sa - sb) + cut(far_s) * lh_s), 1)
            sb_e = cut(near_e) * sa_e - cut(p_1e) * (last / ge8 - cut(far_e) * lh)
            sweep(ge8 * ge8 * (cut(ux) * sa_e - hx8 * sb_e + pm8 * la - (e * pm8 + cut(g) * cut(p_e)) * lh), -1)
            for x in range(BX):
                fbuf[k, x, lo:lo + 8, :] = line[x]

    def mix(x, carry):
        for k in range(KLOC):
            fh, fl = split(fbuf[k, x])
            fcat = jnp.concatenate([fh, fl, fh], axis=0)
            out[k, pl.ds(x, LEV, stride=BX), :] = dot(mcat, fcat, NN)
        return carry

    lax.fori_loop(0, BX, mix, 0, unroll=8)


def per_device(members, gradient, control, filter_rates, vertical_weights, band_widths):
    hbm = pl.BlockSpec(memory_space=pltpu.HBM)
    dma = pltpu.SemaphoreType.DMA

    def vm(*shape):
        return pltpu.VMEM(shape, F32)

    three = [dma((3,))] * 2
    single = [dma] * 2
    out = pl.pallas_call(
        kernel,
        out_shape=pltpu.VMEM((KLOC, ROWS, BY), F32),
        in_specs=[hbm] * 5,
        out_specs=pl.BlockSpec(memory_space=pltpu.VMEM),
        scratch_shapes=[
            pltpu.SMEM((LEV,), F32),
            pltpu.VMEM((1, LEV), jnp.int32),
            vm(LEV, LEV),
            pltpu.VMEM((KLOC, ROWS, BY), BF16),
            vm(ROWS, BY),
            vm(ROWS, BY), vm(ROWS, BY), vm(3, QUARTER, BY),
            vm(KLOC, ROWS, BY), vm(KLOC, ROWS, BY),
            vm(LEV * 8, 128), vm(LEV, 128),
            pltpu.VMEM((LEV * BY, BY), BF16),
            pltpu.VMEM((LEV * BY, BY), BF16),
            vm(GROUPS * 8, 128),
            vm(2, GROUPS, 128), vm(3, 2, GROUPS, 128),
            vm(4, LEV, 128), vm(4, LEV, 128), vm(4, LEV, 128), vm(4, LEV, 128),
            vm(4, GROUPS, 128), vm(3, 2, GROUPS, 128), vm(4, GROUPS, 128), vm(4, GROUPS, 128),
            vm(GROUPS * 8, 128),
            vm(KLOC, 4, LEV, 128), vm(4, LEV, 128),
            vm(2, 2, LEV, 128), vm(2, 2, LEV, 128), vm(2, 2, LEV, 128), vm(2, 2, LEV, 128),
            vm(GROUPS, 128), vm(GROUPS, 128), vm(2, 8, 128), vm(7, 8, 128),
            vm(8 * LEV, 128), vm(8 * LEV, 128),
            vm(KLOC, BX, LEV, BY),
            dma((5,)),
            *three, *three, *three, dma((2, 2, PARTS)), dma((2, 2, PARTS)), *three,
            *single, dma((PARTS,)), dma((PARTS,)),
            dma((2, CHUNKS)), dma((2, CHUNKS)), dma((2,)), dma((2,)),
            dma((7,)), dma((7,)), *single,
        ],
        compiler_params=pltpu.CompilerParams(
            collective_id=0, has_side_effects=True, vmem_limit_bytes=48 << 20),
        name="localize",
    )(*[
        pltpu.with_memory_space_constraint(v, pltpu.HBM)
        for v in (filter_rates, band_widths.reshape(1, LEV), vertical_weights,
                  members.reshape(KLOC, ROWS, BY), gradient.reshape(ROWS, BY))
    ])
    return out.reshape(KLOC, LEV, BX, BY) + control.astype(F32)


def solution(mesh):
    placed = (
        P("mem", None, "gx", "gy"),
        P(None, "gx", "gy"),
        P("mem", None, "gx", "gy"),
        P(),
        P(),
        P(),
    )
    return jax.shard_map(
        per_device,
        mesh=mesh,
        in_specs=placed,
        out_specs=P("mem", None, "gx", "gy"),
        check_vma=False,
    )
```

```python
import functools

import jax
import jax.numpy as jnp
from jax import lax
from jax.experimental import pallas as pl
from jax.experimental.pallas import tpu as pltpu
from jax.sharding import PartitionSpec as P

MESH = pl.DeviceIdType.MESH
F32 = jnp.float32
BF16 = jnp.bfloat16

LEV, MEMBERS, NX, NY = 64, 8, 256, 1024
MEM, GX, GY = 4, 16, 8
KLOC = MEMBERS // MEM
BX, BY = NX // GX, NY // GY
ROWS = LEV * BX
GROUPS = LEV // 4
QUARTER = ROWS // MEM
CHUNKS = 4
CHUNK = LEV // CHUNKS
PARTS = 2
PART = LEV // PARTS

NT = (((1,), (1,)), ((), ()))
NN = (((1,), (0,)), ((), ()))
TN = (((0,), (0,)), ((), ()))


def dot(a, b, dims):
    return lax.dot_general(a, b, dims, preferred_element_type=F32)


def split(x):
    hi = x.astype(BF16)
    return hi, (x - hi.astype(F32)).astype(BF16)


def iota(shape, axis):
    return lax.broadcasted_iota(jnp.int32, shape, axis)


def log_decay(r):
    return -r * (1.0 + r * (0.5 + r * (1.0 / 3 + r * (0.25 + r * (0.2 + r * (1.0 / 6))))))


class Line:
    def __init__(self, rate, total, size, index):
        r = rate
        self.rate = r
        self.log = log_decay(r)
        self.a = 1.0 - r
        self.g = self.a * self.a / (r * (1.0 + self.a))
        self.s = (index * size).astype(F32)
        self.last = self.s + (size - 1.0)
        self.n2 = 2.0 * total - self.last
        self.p_s = self.power(self.s)
        self.p_inv = self.power(-self.last)
        self.p_n2 = self.power(self.n2)
        self.ga = self.g * self.power(2.0 * total)
        self.G = 1.0 + 2.0 * self.g + self.ga
        self.total = total
        self.e = self.s + size

    def reach(self, t):
        near = t + self.g + self.ga - self.g * self.power(2.0 * (self.total - t))
        far = self.g * (self.power(-t - 1.0) - self.power(t - 1.0))
        return near, far

    def power(self, m):
        return jnp.exp(self.log * m)

    def sums(self, r1, r2, q1, q2):
        sa = self.p_inv * r1
        fq = self.p_s * q1
        sb = self.p_inv * (self.last * r1 - r2) + self.g * fq
        lh = fq - self.p_n2 * r1
        la = self.p_s * ((self.s + self.G) * q1 + q2) - self.p_n2 * ((self.n2 + self.G) * r1 + r2)
        return sa, sb, la, lh


def kernel(rates_h, bands_h, weights_h, members, gradient, out,
           rates, bands, weights, mem_v, grad_v, psum, total, rs_rcv, vbuf, zbuf, wtab, lsub, thi, tlo,
           mu, ysum, yone, xsum, xrs, xmn, xrt, ysnd, yrcv, zsnd, zrcv, kap, xst, xpair, xin, xout, xss, xsr,
           cown, csib, ctot, crcv, xr, xf, fbuf,
           in_sem, rs_s, rs_r, ag_s, ag_r, o_s, o_r, xs_s, xs_r, y_s, y_r, h_s, h_r, p_s, p_r,
           c_s, c_r, d_s, d_r, k_s, k_r, l_s, l_r):
    i = lax.axis_index("mem")
    gx = lax.axis_index("gx")
    gy = lax.axis_index("gy")
    z, core = gx // 2, gx % 2
    yy, hh = gy // 2, gy % 2

    barrier = pltpu.get_barrier_semaphore()

    def signal(dev):
        pl.semaphore_signal(barrier, inc=1, device_id=dev, device_id_type=MESH)

    sibling = (i, gx + 1 - 2 * core, gy)
    across = (i, gx, gy + 1 - 2 * hh)
    peers = [((i + d) % MEM, gx, gy) for d in range(1, MEM)]
    y_at = [(yy + d) % 4 for d in range(1, 4)]
    chips = [(i, ((z + d) % 8) * 2 + core, gy) for d in range(1, 8)]
    signal(across)
    for dev in chips[2:5] + chips[1:2] + chips[5:6] + chips[0:1] + chips[6:7]:
        signal(dev)
    for d in range(3):
        signal(peers[d])
        signal((i, gx, y_at[d] * 2 + hh))
    signal(sibling)

    loads = [
        pltpu.make_async_copy(rates_h, rates, in_sem.at[0]),
        pltpu.make_async_copy(members, mem_v, in_sem.at[1]),
        pltpu.make_async_copy(gradient, grad_v, in_sem.at[2]),
        pltpu.make_async_copy(weights_h, weights, in_sem.at[3]),
        pltpu.make_async_copy(bands_h, bands, in_sem.at[4]),
    ]
    for load in loads:
        load.start()

    def remote(src, dst, ss, rs, dev):
        return pltpu.make_async_remote_copy(
            src_ref=src, dst_ref=dst, send_sem=ss, recv_sem=rs, device_id=dev, device_id_type=MESH)

    loads[0].wait()
    sub8 = iota((8, 128), 0)
    for t in range(LEV // 8):
        v = jnp.zeros((8, 128), F32)
        for j in range(8):
            v = jnp.where(sub8 == j, rates[t * 8 + j], v)
        lsub[t * 8:(t + 1) * 8, :] = v
    lane = iota((GROUPS, 128), 1)
    lev_id = iota((GROUPS, 128), 0) * 4 + (lane // BX) % 4
    rate_lane = jnp.zeros((GROUPS, 128), F32)
    for l in range(LEV):
        rate_lane = jnp.where(lev_id == l, rates[l], rate_lane)
    ly = Line(rate_lane, NY, BY, gy)
    lx = Line(lsub[...], NX, BX, gx)
    a_sub = lx.a

    cell = iota((8, 128), 1).astype(F32)
    kind = sub8 % 4
    dist = jnp.where(kind < 2, 127.0 - cell, cell)
    factor = jnp.where(kind % 2 == 0, 1.0, dist)

    def basis(l, carry):
        lg = log_decay(jnp.broadcast_to(lsub[pl.ds(l, 1), :], (8, 128)))
        wtab[pl.ds(pl.multiple_of(l * 8, 8), 8), :] = jnp.exp(dist * lg) * factor
        return carry

    lax.fori_loop(0, LEV, basis, 0, unroll=8)

    loads[1].wait()
    loads[2].wait()
    lane8 = (iota((8, 128), 1) // BX) % 4

    def product(g, carry):
        at = pl.multiple_of(g * 64, 64)
        gr = grad_v[pl.ds(at, 64), :]
        m0 = mem_v[0, pl.ds(at, 64), :].astype(F32)
        m1 = mem_v[1, pl.ds(at, 64), :].astype(F32)
        psum[pl.ds(at, 64), :] = m0 + m1
        v0 = m0 * gr
        v1 = m1 * gr
        vbuf[0, pl.ds(at, 64), :] = v0
        vbuf[1, pl.ds(at, 64), :] = v1
        vh, vl = split(jnp.concatenate([v0, v1], axis=0))
        wh, wl = split(wtab[pl.ds(pl.multiple_of(g * 32, 32), 32), :])
        res = dot(wh, vh, NT) + dot(wh, vl, NT) + dot(wl, vh, NT)
        m8 = jnp.zeros((8, 128), F32)
        for lv in range(4):
            m8 = jnp.where(lane8 == lv, res[lv * 8:lv * 8 + 8, :], m8)
        mu[pl.ds(pl.multiple_of(g * 8, 8), 8), :] = m8
        return carry

    lax.fori_loop(0, GROUPS, product, 0, unroll=GROUPS)
    ymom = [mu[pl.ds(q, GROUPS, stride=8), :] for q in range(4)]
    low = lane < 64
    two = [m + pltpu.roll(m, 64, 1) for m in ymom]
    ysum[0] = jnp.where(low, two[0], two[1])
    ysum[1] = jnp.where(low, two[2], two[3])

    for k in range(KLOC):
        r1 = jnp.zeros((LEV, 128), F32)
        r2, q1, q2 = r1, r1, r1
        for x in range(BX):
            v = vbuf[k, pl.ds(x, LEV, stride=BX), :]
            t = a_sub * r1
            r2 = a_sub * r2 + t
            r1 = t + v
            v = vbuf[k, pl.ds(BX - 1 - x, LEV, stride=BX), :]
            t = a_sub * q1
            q2 = a_sub * q2 + t
            q1 = t + v
        for q, s in enumerate(lx.sums(r1, r2, q1, q2)):
            xst[k, q] = s
            if k == 1:
                xsum[q] = xst[0, q] + s
    pl.semaphore_wait(barrier, 15)
    one = [remote(ysum, yone.at[d], o_s.at[d], o_r.at[d], peers[d]) for d in range(3)]
    for cp in one:
        cp.start()

    ring = [(i + 1 - 2 * (i % 2), gx, gy), (3 - i, gx, gy)]

    def piece(ref, half, c):
        return ref.at[2 * half:2 * half + 2, c * PART:(c + 1) * PART]

    def round_of(step, src, dst):
        return [[remote(piece(src, half, c), piece(dst, half, c), xs_s.at[step, half, c], xs_r.at[step, half, c],
                        ring[(half + step) % 2]) for half in range(2)] for c in range(PARTS)]

    near = round_of(0, xsum, xrs)
    far = round_of(1, xmn, xrt)
    for pair in near:
        for cp in pair:
            cp.start()
    di = jnp.abs(iota((BY, BY), 0) - iota((BY, BY), 1)).astype(F32)

    def toeplitz(l, carry):
        r = jnp.broadcast_to(lsub[pl.ds(l, 1), :], (8, 128))
        lg = log_decay(r)
        a = 1.0 - r
        c = 1.0 + 2.0 * (a * a / (r * (1.0 + a)))
        lg = jnp.broadcast_to(lg[0:1, :], (BY, BY))
        c = jnp.broadcast_to(c[0:1, :], (BY, BY))
        hi, lo = split(jnp.exp(di * lg) * (di + c))
        at = pl.multiple_of(l * BY, BY)
        thi[pl.ds(at, BY), :] = hi
        tlo[pl.ds(at, BY), :] = lo
        return carry

    lax.fori_loop(0, LEV, toeplitz, 0, unroll=2)

    for cp in one:
        cp.wait()
    tot = [ysum[j] + yone[0, j] + yone[1, j] + yone[2, j] for j in range(2)]
    swap = [pltpu.roll(t, 64, 1) for t in tot]
    mean = [jnp.where(low, tot[0], swap[0]), jnp.where(low, swap[0], tot[0]),
            jnp.where(low, tot[1], swap[1]), jnp.where(low, swap[1], tot[1])]
    r1, r2, q1, q2 = [m - t * (1.0 / MEMBERS) for m, t in zip(ymom, mean)]
    own_y = ly.sums(r1, r2, q1, q2)
    for q in range(4):
        ysnd[q] = own_y[q]
    ycp = []
    for d in range(3):
        part = pl.multiple_of(jnp.where(y_at[d] > yy, 0, 2), 2)
        cp = remote(ysnd.at[pl.ds(part, 2)], yrcv.at[d], y_s.at[d], y_r.at[d], (i, gx, y_at[d] * 2 + hh))
        cp.start()
        ycp.append(cp)

    for c in range(PARTS):
        rows = slice(c * PART, (c + 1) * PART)
        for cp in near[c]:
            cp.wait()
        xmn[:, rows] = xsum[:, rows] + xrs[:, rows]
        for cp in far[c]:
            cp.start()
    rs = [remote(psum.at[pl.ds(pl.multiple_of(peers[d][0] * QUARTER, QUARTER), QUARTER)], rs_rcv.at[d],
                 rs_s.at[d], rs_r.at[d], peers[d]) for d in range(3)]
    for cp in rs:
        cp.start()

    for cp in ycp:
        cp.wait()
    zero = jnp.zeros((GROUPS, 128), F32)
    sa = sb = la = lh = zero
    for d in range(3):
        from_left = (yy - (d + 1)) >= 0
        u, w = yrcv[d, 0], yrcv[d, 1]
        sa = sa + jnp.where(from_left, u, 0.0)
        sb = sb + jnp.where(from_left, w, 0.0)
        la = la + jnp.where(from_left, 0.0, u)
        lh = lh + jnp.where(from_left, 0.0, w)
    zsnd[0] = sa + jnp.where(hh == 0, own_y[0], 0.0)
    zsnd[1] = sb + jnp.where(hh == 0, own_y[1], 0.0)
    zsnd[2] = la + jnp.where(hh == 1, own_y[2], 0.0)
    zsnd[3] = lh + jnp.where(hh == 1, own_y[3], 0.0)
    hcp = remote(zsnd, zrcv, h_s, h_r, across)
    hcp.start()

    pcp = []
    for c in range(PARTS):
        rows = slice(c * PART, (c + 1) * PART)
        for cp in far[c]:
            cp.wait()
        for q in range(4):
            m = (xmn[q, rows] + xrt[q, rows]) * (1.0 / MEMBERS)
            for k in range(KLOC):
                xst[k, q, rows] = xst[k, q, rows] - m
        cp = remote(xst.at[1 - core, :, rows], xpair.at[:, rows], p_s.at[c], p_r.at[c], sibling)
        cp.start()
        pcp.append(cp)


    def chain(turn):
        way = ((z >= 4).astype(jnp.int32) + turn) % 2
        has_in = jnp.where(way == 0, z > 0, z < 7)
        has_out = jnp.where(way == 0, z < 7, z > 0)
        target = (i, gx + 2 - 4 * way, gy)
        part = pl.multiple_of(way * 2, 2)

        def copy(c):
            rows = pl.ds(c * CHUNK, CHUNK)
            return remote(xout.at[way, :, rows], xin.at[way, :, rows], c_s.at[way, c], c_r.at[way, c], target)

        @pl.when(jnp.logical_not(has_in))
        def _():
            xin[way] = jnp.zeros((2, LEV, 128), F32)

        for c in range(CHUNKS):
            rows = slice(c * CHUNK, (c + 1) * CHUNK)

            if turn == 0 and c % (CHUNKS // PARTS) == 0:
                pcp[c // (CHUNKS // PARTS)].wait()

            @pl.when(has_in)
            def _():
                copy(c).wait_recv()

            @pl.when(has_out)
            def _():
                xout[way, :, rows] = (xin[way, :, rows] + xst[core, pl.ds(part, 2), rows]
                                      + xpair[pl.ds(part, 2), rows])
                copy(c).start()

        add = jnp.where(way == core, 1.0, 0.0)
        xss[way] = xin[way] + add * xst[core, pl.ds(part, 2)]
        sib = remote(xss.at[way], xsr.at[way], d_s.at[way], d_r.at[way], sibling)
        sib.start()
        xin[way] = xin[way] + (1.0 - add) * xpair[pl.ds(part, 2)]
        return way, has_out, copy, sib

    def drain(done):
        for way, has_out, copy, sib in done:
            sib.wait()
            for c in range(CHUNKS):
                @pl.when(has_out)
                def _():
                    copy(c).wait_send()

    done = [chain(0)]
    own = pl.multiple_of(i * QUARTER, QUARTER)
    for cp in rs:
        cp.wait()
    total[pl.ds(own, QUARTER), :] = (psum[pl.ds(own, QUARTER), :] + rs_rcv[0]
                                     + rs_rcv[1] + rs_rcv[2])
    ag = [remote(total.at[pl.ds(own, QUARTER)], total.at[pl.ds(own, QUARTER)], ag_s.at[d], ag_r.at[d], peers[d])
          for d in range(3)]
    for cp in ag:
        cp.start()

    hcp.wait()
    sa = sa + zrcv[0]
    sb = sb + zrcv[1]
    la = la + zrcv[2]
    lh = lh + zrcv[3]
    k1 = (ly.p_n2 * (sb - sa * (ly.n2 + ly.G)) + ly.p_inv * (la - lh * ly.last)
          + ly.ga * ly.p_inv * (ly.p_s * q1)
          - ly.p_n2 * ly.p_inv * ((2.0 * (NY - ly.last) + ly.G) * r1 + r2))
    k2 = lh * ly.p_inv - sa * ly.p_n2 - ly.p_n2 * ly.p_inv * r1
    k3 = ly.p_s * (sa * (ly.s + ly.G) - sb - lh * ly.g + ly.ga * ly.p_inv * r1 - ly.g * ly.p_s * q1)
    k4 = sa * ly.p_s
    kk = (k1, k2, k3, k4)

    lxl = Line(rate_lane, NX, BX, gx)
    xc = (lane % BX).astype(F32)
    up, down = lxl.power(xc), lxl.power(BX - 1.0 - xc)
    wts = lxl.sums(down, (BX - 1.0 - xc) * down, up, xc * up)
    stack = jnp.concatenate([w * kq for w in wts for kq in kk], axis=0)
    seg = (iota((128, 128), 0) // BX == iota((128, 128), 1) // BX).astype(BF16)
    sh, sl = split(stack)
    res = dot(sh, seg, NN) + dot(sl, seg, NN)
    slot = lane % BX
    slot8 = iota((8, 128), 1) % BX < 8
    cor = zero
    for c in range(16):
        cor = jnp.where(slot == c, res[c * GROUPS:(c + 1) * GROUPS], cor)
    cown[...] = cor
    lcp = remote(cown, csib, l_s, l_r, sibling)
    lcp.start()
    for q, k in enumerate(kk + (zero,) * 4):
        kap[pl.ds(q, GROUPS, stride=8), :] = k

    def spread():
        lcp.wait()
        even = cown[pl.ds(0, 8, stride=2), :] + csib[pl.ds(0, 8, stride=2), :]
        odd = cown[pl.ds(1, 8, stride=2), :] + csib[pl.ds(1, 8, stride=2), :]
        ctot[0] = jnp.where(slot8, even, pltpu.roll(odd, 8, 1))
        ctot[1] = jnp.where(slot8, pltpu.roll(even, 120, 1), odd)
        for d in (3, 2, 4, 1, 5, 0, 6):
            ccp[d].start()

    to_right = [(z + d + 1) <= 7 for d in range(7)]
    ccp = [remote(ctot.at[jnp.where(to_right[d], 0, 1)], crcv.at[d], k_s.at[d], k_r.at[d], chips[d]) for d in range(7)]

    def local_y(l, carry):
        at = pl.multiple_of(l * BX, BX)
        tt = pl.multiple_of(l * BY, BY)
        mean = total[pl.ds(at, BX), :] * (1.0 / MEMBERS)
        gr = grad_v[pl.ds(at, BX), :]
        v = jnp.concatenate([(mem_v[k, pl.ds(at, BX), :].astype(F32) - mean) * gr for k in range(KLOC)], axis=0)
        n = KLOC * BX
        both = jnp.concatenate([thi[pl.ds(tt, BY), :], tlo[pl.ds(tt, BY), :]], axis=1)
        res = dot(jnp.concatenate(split(v), axis=0), both, NN)
        res = res[:n, :BY] + res[n:, :BY] + res[:n, BY:]
        zbuf[0, pl.ds(at, BX), :] = res[0:BX]
        zbuf[1, pl.ds(at, BX), :] = res[BX:]
        return carry

    def synth(g, carry):
        at = pl.multiple_of(g * 64, 64)
        k8 = kap[pl.ds(pl.multiple_of(g * 8, 8), 8), :]
        big = jnp.concatenate([jnp.where(lane8 == lv, k8, 0.0) for lv in range(4)], axis=0)
        kh, kl = split(big)
        wh, wl = split(wtab[pl.ds(pl.multiple_of(g * 32, 32), 32), :])
        res = dot(jnp.concatenate([kh, kl, kh], axis=0), jnp.concatenate([wh, wh, wl], axis=0), TN)
        zbuf[0, pl.ds(at, 64), :] += res[0:64]
        zbuf[1, pl.ds(at, 64), :] += res[64:]
        return carry

    def block():
        for cp in ag:
            cp.wait()
        lax.fori_loop(0, LEV, local_y, 0, unroll=8)
        lax.fori_loop(0, GROUPS, synth, 0, unroll=4)

    middle = (z >= 1) & (z <= 6)
    centre = (z == 3) | (z == 4)

    @pl.when(jnp.logical_not(centre))
    def _():
        spread()

    for load in loads[3:5]:
        load.wait()
    alpha = lx.rate / (1.0 + a_sub)
    scale = 2.0 * lx.rate * lx.rate * lx.rate * alpha * alpha
    pid = iota((LEV, LEV), 0)
    lid = iota((LEV, LEV), 1)
    keep = jnp.abs(pid - lid) <= bands[...]
    mixed = jnp.where(keep, weights[...], 0.0) * scale[:, 0:LEV]
    mh, ml = split(mixed.T)
    mcat = jnp.concatenate([mh, mh, ml], axis=1)

    def rest():
        block()

    @pl.when(jnp.logical_not(middle))
    def _():
        rest()

    done.append(chain(1))

    @pl.when(centre)
    def _():
        spread()

    @pl.when(middle)
    def _():
        rest()

    drain(done)

    for k in range(KLOC):
        for q in range(4):
            row = (k * 4 + q) * LEV
            xr[row:row + LEV, :] = jnp.where(core == k, xin[q // 2, q % 2], xsr[q // 2, q % 2])

    def local_x(l, carry):
        tt = pl.multiple_of(l * BY, BY)
        vh, vl = split(xr[pl.ds(l, 8, stride=LEV), :])
        th = thi[pl.ds(tt, BY), :]
        xf[pl.ds(l, 8, stride=LEV), :] = dot(jnp.concatenate([vh, vl, vh], axis=1),
                                             jnp.concatenate([th, th, tlo[pl.ds(tt, BY), :]], axis=0), NN)
        return carry

    lax.fori_loop(0, LEV, local_x, 0, unroll=16)
    for cp in ccp:
        cp.wait()
    to_me, to_us = jnp.zeros((8, 128), F32), jnp.zeros((8, 128), F32)
    for d in range(7):
        from_left = (z - (d + 1)) >= 0
        to_me = to_me + jnp.where(from_left, crcv[d], 0.0)
        to_us = to_us + jnp.where(from_left, 0.0, crcv[d])
    mate = jnp.where((slot < 8) == (core == 1), csib[...], 0.0)
    cown[...] = mate
    cown[pl.ds(0, 8, stride=2), :] += jnp.where(slot8, to_me, pltpu.roll(to_us, 8, 1))
    cown[pl.ds(1, 8, stride=2), :] += jnp.where(slot8, pltpu.roll(to_me, 120, 1), to_us)
    zr, zc = iota((64, 256), 0), iota((64, 256), 1)
    fits = ((zr // 32 == (zc // 64) % 2) & ((zr // 8) % 4 == (zc // 4) % 4)
            & ((zr % 8) // 4 == zc // 128) & (zr % 4 == (zc // 16) % 4))

    def synth_x(t, carry):
        row = jnp.concatenate([cown[pl.ds(2 * t, 1), :], cown[pl.ds(2 * t + 1, 1), :]], axis=1)
        kh, kl = split(jnp.where(fits, jnp.broadcast_to(row, (64, 256)), 0.0))
        w = wtab[pl.ds(pl.multiple_of(t * 64, 64), 64), :]
        tiles = [w[(g * 4 + lv) * 8:(g * 4 + lv) * 8 + 8] for g in range(2) for k in range(2)
                 for lv in range(4) for twice in range(2)]
        wh, wl = split(jnp.concatenate(tiles, axis=0))
        res = dot(kh, wh, NN) + dot(kl, wh, NN) + dot(kh, wl, NN)
        for j in range(8):
            xf[pl.ds(pl.multiple_of(j * LEV + t * 8, 8), 8), :] += res[j * 8:(j + 1) * 8]
        return carry

    lax.fori_loop(0, LEV // 8, synth_x, 0, unroll=8)

    g, s, e, G = lx.g, lx.s, lx.e, lx.G
    ge = 1.0 + g
    p_s, p_e, p_me, p_2e = lx.power(s), lx.power(e), lx.power(-e), lx.power(2.0 * NX - e)
    hx = p_e - p_2e
    ux = p_e * (e + G) - p_2e * (2.0 * NX - e + G)
    hs = p_s - lx.power(2.0 * NX - s)
    p_s1, p_1e = lx.power(s - 1.0), lx.power(1.0 - e)
    near_s, far_s = lx.reach(s)
    near_e, far_e = lx.reach(e)

    for k in range(KLOC):
        for t in range(LEV // 8):
            lo = t * 8
            cut = lambda m: m[lo:lo + 8]
            sa, sb, la, lh = [xf[(k * 4 + q) * LEV + lo:(k * 4 + q) * LEV + lo + 8, :] for q in range(4)]
            a8, ge8, hx8, pm8 = cut(a_sub), cut(ge), cut(hx), cut(p_me)
            line = [zbuf[k, pl.ds(lo * BX + x, 8, stride=BX), :] for x in range(BX)]

            def sweep(run, order):
                for x in range(BX)[::order]:
                    run = a8 * run + line[x]
                    line[x] = run
                return run

            sa_e = cut(p_1e) * sweep(cut(p_s1) * sa, 1)
            first = sweep(ge8 * (hx8 * sa_e + pm8 * lh), -1)
            lh_s = cut(p_s) * (first / ge8 - cut(hs) * sa)
            last = sweep(ge8 * (cut(p_s1) * (cut(near_s) * sa - sb) + cut(far_s) * lh_s), 1)
            sb_e = cut(near_e) * sa_e - cut(p_1e) * (last / ge8 - cut(far_e) * lh)
            sweep(ge8 * ge8 * (cut(ux) * sa_e - hx8 * sb_e + pm8 * la - (e * pm8 + cut(g) * cut(p_e)) * lh), -1)
            for x in range(BX):
                fbuf[k, x, lo:lo + 8, :] = line[x]

    def mix(x, carry):
        for k in range(KLOC):
            fh, fl = split(fbuf[k, x])
            fcat = jnp.concatenate([fh, fl, fh], axis=0)
            out[k, pl.ds(x, LEV, stride=BX), :] = dot(mcat, fcat, NN)
        return carry

    lax.fori_loop(0, BX, mix, 0, unroll=8)


def per_device(members, gradient, control, filter_rates, vertical_weights, band_widths):
    hbm = pl.BlockSpec(memory_space=pltpu.HBM)
    dma = pltpu.SemaphoreType.DMA

    def vm(*shape):
        return pltpu.VMEM(shape, F32)

    three = [dma((3,))] * 2
    single = [dma] * 2
    out = pl.pallas_call(
        kernel,
        out_shape=pltpu.VMEM((KLOC, ROWS, BY), F32),
        in_specs=[hbm] * 5,
        out_specs=pl.BlockSpec(memory_space=pltpu.VMEM),
        scratch_shapes=[
            pltpu.SMEM((LEV,), F32),
            pltpu.VMEM((1, LEV), jnp.int32),
            vm(LEV, LEV),
            pltpu.VMEM((KLOC, ROWS, BY), BF16),
            vm(ROWS, BY),
            vm(ROWS, BY), vm(ROWS, BY), vm(3, QUARTER, BY),
            vm(KLOC, ROWS, BY), vm(KLOC, ROWS, BY),
            vm(LEV * 8, 128), vm(LEV, 128),
            pltpu.VMEM((LEV * BY, BY), BF16),
            pltpu.VMEM((LEV * BY, BY), BF16),
            vm(GROUPS * 8, 128),
            vm(2, GROUPS, 128), vm(3, 2, GROUPS, 128),
            vm(4, LEV, 128), vm(4, LEV, 128), vm(4, LEV, 128), vm(4, LEV, 128),
            vm(4, GROUPS, 128), vm(3, 2, GROUPS, 128), vm(4, GROUPS, 128), vm(4, GROUPS, 128),
            vm(GROUPS * 8, 128),
            vm(KLOC, 4, LEV, 128), vm(4, LEV, 128),
            vm(2, 2, LEV, 128), vm(2, 2, LEV, 128), vm(2, 2, LEV, 128), vm(2, 2, LEV, 128),
            vm(GROUPS, 128), vm(GROUPS, 128), vm(2, 8, 128), vm(7, 8, 128),
            vm(8 * LEV, 128), vm(8 * LEV, 128),
            vm(KLOC, BX, LEV, BY),
            dma((5,)),
            *three, *three, *three, dma((2, 2, PARTS)), dma((2, 2, PARTS)), *three,
            *single, dma((PARTS,)), dma((PARTS,)),
            dma((2, CHUNKS)), dma((2, CHUNKS)), dma((2,)), dma((2,)),
            dma((7,)), dma((7,)), *single,
        ],
        compiler_params=pltpu.CompilerParams(
            collective_id=0, has_side_effects=True, vmem_limit_bytes=48 << 20),
        name="localize",
    )(*[
        pltpu.with_memory_space_constraint(v, pltpu.HBM)
        for v in (filter_rates, band_widths.reshape(1, LEV), vertical_weights,
                  members.reshape(KLOC, ROWS, BY), gradient.reshape(ROWS, BY))
    ])
    return out.reshape(KLOC, LEV, BX, BY) + control.astype(F32)


def solution(mesh):
    placed = (
        P("mem", None, "gx", "gy"),
        P(None, "gx", "gy"),
        P("mem", None, "gx", "gy"),
        P(),
        P(),
        P(),
    )
    return jax.shard_map(
        per_device,
        mesh=mesh,
        in_specs=placed,
        out_specs=P("mem", None, "gx", "gy"),
        check_vma=False,
    )
```

```python
import functools

import jax
import jax.numpy as jnp
from jax import lax
from jax.experimental import pallas as pl
from jax.experimental.pallas import tpu as pltpu
from jax.sharding import PartitionSpec as P

MESH = pl.DeviceIdType.MESH
F32 = jnp.float32
BF16 = jnp.bfloat16

LEV, MEMBERS, NX, NY = 64, 8, 256, 1024
MEM, GX, GY = 4, 16, 8
KLOC = MEMBERS // MEM
BX, BY = NX // GX, NY // GY
ROWS = LEV * BX
GROUPS = LEV // 4
QUARTER = ROWS // MEM
PARTS = 2
PART = LEV // PARTS

NT = (((1,), (1,)), ((), ()))
NN = (((1,), (0,)), ((), ()))
TN = (((0,), (0,)), ((), ()))


def dot(a, b, dims):
    return lax.dot_general(a, b, dims, preferred_element_type=F32)


def split(x):
    hi = x.astype(BF16)
    return hi, (x - hi.astype(F32)).astype(BF16)


def iota(shape, axis):
    return lax.broadcasted_iota(jnp.int32, shape, axis)


def log_decay(r):
    return -r * (1.0 + r * (0.5 + r * (1.0 / 3 + r * (0.25 + r * (0.2 + r * (1.0 / 6))))))


class Line:
    def __init__(self, rate, total, size, index):
        r = rate
        self.rate = r
        self.log = log_decay(r)
        self.a = 1.0 - r
        self.g = self.a * self.a / (r * (1.0 + self.a))
        self.s = (index * size).astype(F32)
        self.last = self.s + (size - 1.0)
        self.n2 = 2.0 * total - self.last
        self.p_s = self.power(self.s)
        self.p_inv = self.power(-self.last)
        self.p_n2 = self.power(self.n2)
        self.ga = self.g * self.power(2.0 * total)
        self.G = 1.0 + 2.0 * self.g + self.ga
        self.total = total
        self.e = self.s + size

    def reach(self, t):
        near = t + self.g + self.ga - self.g * self.power(2.0 * (self.total - t))
        far = self.g * (self.power(-t - 1.0) - self.power(t - 1.0))
        return near, far

    def power(self, m):
        return jnp.exp(self.log * m)

    def sums(self, r1, r2, q1, q2):
        sa = self.p_inv * r1
        fq = self.p_s * q1
        sb = self.p_inv * (self.last * r1 - r2) + self.g * fq
        lh = fq - self.p_n2 * r1
        la = self.p_s * ((self.s + self.G) * q1 + q2) - self.p_n2 * ((self.n2 + self.G) * r1 + r2)
        return sa, sb, la, lh


def kernel(rates_h, bands_h, weights_h, members, gradient, out,
           rates, bands, weights, mem_v, grad_v, psum, total, rs_rcv, vbuf, zbuf, wtab, lsub, thi, tlo,
           mu, ysum, yone, xsum, xrs, xmn, xrt, ysnd, yrcv, zsnd, zrcv, kap, xst, xpair, xin, xout, xlo, xss, xsr,
           cown, csib, ctot, crcv, xr, xf, fbuf,
           in_sem, rs_s, rs_r, ag_s, ag_r, o_s, o_r, xs_s, xs_r, y_s, y_r, h_s, h_r, p_s, p_r,
           c_s, c_r, d_s, d_r, k_s, k_r, l_s, l_r):
    i = lax.axis_index("mem")
    gx = lax.axis_index("gx")
    gy = lax.axis_index("gy")
    z, core = gx // 2, gx % 2
    yy, hh = gy // 2, gy % 2

    barrier = pltpu.get_barrier_semaphore()

    def signal(dev):
        pl.semaphore_signal(barrier, inc=1, device_id=dev, device_id_type=MESH)

    sibling = (i, gx + 1 - 2 * core, gy)
    across = (i, gx, gy + 1 - 2 * hh)
    peers = [((i + d) % MEM, gx, gy) for d in range(1, MEM)]
    y_at = [(yy + d) % 4 for d in range(1, 4)]
    chips = [(i, ((z + d) % 8) * 2 + core, gy) for d in range(1, 8)]
    signal(across)
    for dev in chips[2:5] + chips[1:2] + chips[5:6] + chips[0:1] + chips[6:7]:
        signal(dev)
    for d in range(3):
        signal(peers[d])
        signal((i, gx, y_at[d] * 2 + hh))
    signal(sibling)

    loads = [
        pltpu.make_async_copy(rates_h, rates, in_sem.at[0]),
        pltpu.make_async_copy(members, mem_v, in_sem.at[1]),
        pltpu.make_async_copy(gradient, grad_v, in_sem.at[2]),
        pltpu.make_async_copy(weights_h, weights, in_sem.at[3]),
        pltpu.make_async_copy(bands_h, bands, in_sem.at[4]),
    ]
    for load in loads:
        load.start()

    def remote(src, dst, ss, rs, dev):
        return pltpu.make_async_remote_copy(
            src_ref=src, dst_ref=dst, send_sem=ss, recv_sem=rs, device_id=dev, device_id_type=MESH)

    loads[0].wait()
    sub8 = iota((8, 128), 0)
    for t in range(LEV // 8):
        v = jnp.zeros((8, 128), F32)
        for j in range(8):
            v = jnp.where(sub8 == j, rates[t * 8 + j], v)
        lsub[t * 8:(t + 1) * 8, :] = v
    lane = iota((GROUPS, 128), 1)
    lev_id = iota((GROUPS, 128), 0) * 4 + (lane // BX) % 4
    rate_lane = jnp.zeros((GROUPS, 128), F32)
    for l in range(LEV):
        rate_lane = jnp.where(lev_id == l, rates[l], rate_lane)
    ly = Line(rate_lane, NY, BY, gy)
    lx = Line(lsub[...], NX, BX, gx)
    a_sub = lx.a

    cell = iota((8, 128), 1).astype(F32)
    kind = sub8 % 4
    dist = jnp.where(kind < 2, 127.0 - cell, cell)
    factor = jnp.where(kind % 2 == 0, 1.0, dist)

    def basis(l, carry):
        lg = log_decay(jnp.broadcast_to(lsub[pl.ds(l, 1), :], (8, 128)))
        wtab[pl.ds(pl.multiple_of(l * 8, 8), 8), :] = jnp.exp(dist * lg) * factor
        return carry

    lax.fori_loop(0, LEV, basis, 0, unroll=8)

    loads[1].wait()
    loads[2].wait()
    lane8 = (iota((8, 128), 1) // BX) % 4

    def product(g, carry):
        at = pl.multiple_of(g * 64, 64)
        gr = grad_v[pl.ds(at, 64), :]
        m0 = mem_v[0, pl.ds(at, 64), :].astype(F32)
        m1 = mem_v[1, pl.ds(at, 64), :].astype(F32)
        psum[pl.ds(at, 64), :] = m0 + m1
        v0 = m0 * gr
        v1 = m1 * gr
        vbuf[0, pl.ds(at, 64), :] = v0
        vbuf[1, pl.ds(at, 64), :] = v1
        vh, vl = split(jnp.concatenate([v0, v1], axis=0))
        wh, wl = split(wtab[pl.ds(pl.multiple_of(g * 32, 32), 32), :])
        res = dot(wh, vh, NT) + dot(wh, vl, NT) + dot(wl, vh, NT)
        m8 = jnp.zeros((8, 128), F32)
        for lv in range(4):
            m8 = jnp.where(lane8 == lv, res[lv * 8:lv * 8 + 8, :], m8)
        mu[pl.ds(pl.multiple_of(g * 8, 8), 8), :] = m8
        return carry

    lax.fori_loop(0, GROUPS, product, 0, unroll=GROUPS)
    ymom = [mu[pl.ds(q, GROUPS, stride=8), :] for q in range(4)]
    low = lane < 64
    two = [m + pltpu.roll(m, 64, 1) for m in ymom]
    ysum[0] = jnp.where(low, two[0], two[1])
    ysum[1] = jnp.where(low, two[2], two[3])

    for k in range(KLOC):
        r1 = jnp.zeros((LEV, 128), F32)
        r2, q1, q2 = r1, r1, r1
        for x in range(BX):
            v = vbuf[k, pl.ds(x, LEV, stride=BX), :]
            t = a_sub * r1
            r2 = a_sub * r2 + t
            r1 = t + v
            v = vbuf[k, pl.ds(BX - 1 - x, LEV, stride=BX), :]
            t = a_sub * q1
            q2 = a_sub * q2 + t
            q1 = t + v
        for q, s in enumerate(lx.sums(r1, r2, q1, q2)):
            xst[k, q] = s
            if k == 1:
                xsum[q] = xst[0, q] + s
    pl.semaphore_wait(barrier, 15)
    one = [remote(ysum, yone.at[d], o_s.at[d], o_r.at[d], peers[d]) for d in range(3)]
    for cp in one:
        cp.start()

    ring = [(i + 1 - 2 * (i % 2), gx, gy), (3 - i, gx, gy)]

    def piece(ref, half, c):
        return ref.at[2 * half:2 * half + 2, c * PART:(c + 1) * PART]

    def round_of(step, src, dst):
        return [[remote(piece(src, half, c), piece(dst, half, c), xs_s.at[step, half, c], xs_r.at[step, half, c],
                        ring[(half + step) % 2]) for half in range(2)] for c in range(PARTS)]

    near = round_of(0, xsum, xrs)
    far = round_of(1, xmn, xrt)
    for pair in near:
        for cp in pair:
            cp.start()
    di = jnp.abs(iota((BY, BY), 0) - iota((BY, BY), 1)).astype(F32)

    def toeplitz(l, carry):
        r = jnp.broadcast_to(lsub[pl.ds(l, 1), :], (8, 128))
        lg = log_decay(r)
        a = 1.0 - r
        c = 1.0 + 2.0 * (a * a / (r * (1.0 + a)))
        lg = jnp.broadcast_to(lg[0:1, :], (BY, BY))
        c = jnp.broadcast_to(c[0:1, :], (BY, BY))
        hi, lo = split(jnp.exp(di * lg) * (di + c))
        at = pl.multiple_of(l * BY, BY)
        thi[pl.ds(at, BY), :] = hi
        tlo[pl.ds(at, BY), :] = lo
        return carry

    lax.fori_loop(0, LEV, toeplitz, 0, unroll=2)

    for cp in one:
        cp.wait()
    tot = [ysum[j] + yone[0, j] + yone[1, j] + yone[2, j] for j in range(2)]
    swap = [pltpu.roll(t, 64, 1) for t in tot]
    mean = [jnp.where(low, tot[0], swap[0]), jnp.where(low, swap[0], tot[0]),
            jnp.where(low, tot[1], swap[1]), jnp.where(low, swap[1], tot[1])]
    r1, r2, q1, q2 = [m - t * (1.0 / MEMBERS) for m, t in zip(ymom, mean)]
    own_y = ly.sums(r1, r2, q1, q2)
    for q in range(4):
        ysnd[q] = own_y[q]
    ycp = []
    for d in range(3):
        part = pl.multiple_of(jnp.where(y_at[d] > yy, 0, 2), 2)
        cp = remote(ysnd.at[pl.ds(part, 2)], yrcv.at[d], y_s.at[d], y_r.at[d], (i, gx, y_at[d] * 2 + hh))
        cp.start()
        ycp.append(cp)

    for c in range(PARTS):
        rows = slice(c * PART, (c + 1) * PART)
        for cp in near[c]:
            cp.wait()
        xmn[:, rows] = xsum[:, rows] + xrs[:, rows]
        for cp in far[c]:
            cp.start()
    rs = [remote(psum.at[pl.ds(pl.multiple_of(peers[d][0] * QUARTER, QUARTER), QUARTER)], rs_rcv.at[d],
                 rs_s.at[d], rs_r.at[d], peers[d]) for d in range(3)]
    for cp in rs:
        cp.start()

    for cp in ycp:
        cp.wait()
    zero = jnp.zeros((GROUPS, 128), F32)
    sa = sb = la = lh = zero
    for d in range(3):
        from_left = (yy - (d + 1)) >= 0
        u, w = yrcv[d, 0], yrcv[d, 1]
        sa = sa + jnp.where(from_left, u, 0.0)
        sb = sb + jnp.where(from_left, w, 0.0)
        la = la + jnp.where(from_left, 0.0, u)
        lh = lh + jnp.where(from_left, 0.0, w)
    zsnd[0] = sa + jnp.where(hh == 0, own_y[0], 0.0)
    zsnd[1] = sb + jnp.where(hh == 0, own_y[1], 0.0)
    zsnd[2] = la + jnp.where(hh == 1, own_y[2], 0.0)
    zsnd[3] = lh + jnp.where(hh == 1, own_y[3], 0.0)
    hcp = remote(zsnd, zrcv, h_s, h_r, across)
    hcp.start()

    pcp = []
    for c in range(PARTS):
        rows = slice(c * PART, (c + 1) * PART)
        for cp in far[c]:
            cp.wait()
        for q in range(4):
            m = (xmn[q, rows] + xrt[q, rows]) * (1.0 / MEMBERS)
            for k in range(KLOC):
                xst[k, q, rows] = xst[k, q, rows] - m
        cp = remote(xst.at[1 - core, :, rows], xpair.at[:, rows], p_s.at[c], p_r.at[c], sibling)
        cp.start()
        pcp.append(cp)


    def comes(r, way):
        return z >= (1 << r) if way == 0 else z + (1 << r) <= 7

    def leaves(r, way):
        return z + (1 << r) <= 7 if way == 0 else z >= (1 << r)

    def hop(r, way, c):
        rows = pl.ds(c * PART, PART)
        step = (2 << r) * (1 - 2 * way)
        return remote(xout.at[r, way, :, rows], xin.at[r, way, :, rows], c_s.at[r, way, c], c_r.at[r, way, c],
                      (i, gx + step, gy))

    for r in range(3):
        for way in range(2):
            @pl.when(jnp.logical_not(comes(r, way)))
            def _():
                xin[r, way] = jnp.zeros((2, LEV, 128), F32)

    def rounds(r):
        for c in range(PARTS):
            rows = slice(c * PART, (c + 1) * PART)
            if r == 0:
                pcp[c].wait()
            for way in range(2):
                if r == 0:
                    xout[0, way, :, rows] = xst[core, 2 * way:2 * way + 2, rows] + xpair[2 * way:2 * way + 2, rows]
                else:
                    @pl.when(comes(r - 1, way))
                    def _():
                        hop(r - 1, way, c).wait_recv()

                    xout[r, way, :, rows] = xout[r - 1, way, :, rows] + xin[r - 1, way, :, rows]

                @pl.when(leaves(r, way))
                def _():
                    hop(r, way, c).start()

    def collect():
        sibs = []
        for way in range(2):
            for c in range(PARTS):
                @pl.when(comes(2, way))
                def _():
                    hop(2, way, c).wait_recv()

            before = xin[0, way] + xin[1, way] + xin[2, way]
            add = jnp.where(way == core, 1.0, 0.0)
            xss[way] = before + add * xst[core, 2 * way:2 * way + 2]
            sib = remote(xss.at[way], xsr.at[way], d_s.at[way], d_r.at[way], sibling)
            sib.start()
            sibs.append(sib)
            xlo[way] = before + (1.0 - add) * xpair[2 * way:2 * way + 2]
        for sib in sibs:
            sib.wait()
        for r in range(3):
            for way in range(2):
                for c in range(PARTS):
                    @pl.when(leaves(r, way))
                    def _():
                        hop(r, way, c).wait_send()

    rounds(0)
    rounds(1)
    own = pl.multiple_of(i * QUARTER, QUARTER)
    for cp in rs:
        cp.wait()
    total[pl.ds(own, QUARTER), :] = (psum[pl.ds(own, QUARTER), :] + rs_rcv[0]
                                     + rs_rcv[1] + rs_rcv[2])
    ag = [remote(total.at[pl.ds(own, QUARTER)], total.at[pl.ds(own, QUARTER)], ag_s.at[d], ag_r.at[d], peers[d])
          for d in range(3)]
    for cp in ag:
        cp.start()

    hcp.wait()
    sa = sa + zrcv[0]
    sb = sb + zrcv[1]
    la = la + zrcv[2]
    lh = lh + zrcv[3]
    k1 = (ly.p_n2 * (sb - sa * (ly.n2 + ly.G)) + ly.p_inv * (la - lh * ly.last)
          + ly.ga * ly.p_inv * (ly.p_s * q1)
          - ly.p_n2 * ly.p_inv * ((2.0 * (NY - ly.last) + ly.G) * r1 + r2))
    k2 = lh * ly.p_inv - sa * ly.p_n2 - ly.p_n2 * ly.p_inv * r1
    k3 = ly.p_s * (sa * (ly.s + ly.G) - sb - lh * ly.g + ly.ga * ly.p_inv * r1 - ly.g * ly.p_s * q1)
    k4 = sa * ly.p_s
    kk = (k1, k2, k3, k4)

    lxl = Line(rate_lane, NX, BX, gx)
    xc = (lane % BX).astype(F32)
    up, down = lxl.power(xc), lxl.power(BX - 1.0 - xc)
    wts = lxl.sums(down, (BX - 1.0 - xc) * down, up, xc * up)
    stack = jnp.concatenate([w * kq for w in wts for kq in kk], axis=0)
    seg = (iota((128, 128), 0) // BX == iota((128, 128), 1) // BX).astype(BF16)
    sh, sl = split(stack)
    res = dot(sh, seg, NN) + dot(sl, seg, NN)
    slot = lane % BX
    slot8 = iota((8, 128), 1) % BX < 8
    cor = zero
    for c in range(16):
        cor = jnp.where(slot == c, res[c * GROUPS:(c + 1) * GROUPS], cor)
    cown[...] = cor
    lcp = remote(cown, csib, l_s, l_r, sibling)
    lcp.start()
    for q, k in enumerate(kk + (zero,) * 4):
        kap[pl.ds(q, GROUPS, stride=8), :] = k

    def spread():
        lcp.wait()
        even = cown[pl.ds(0, 8, stride=2), :] + csib[pl.ds(0, 8, stride=2), :]
        odd = cown[pl.ds(1, 8, stride=2), :] + csib[pl.ds(1, 8, stride=2), :]
        ctot[0] = jnp.where(slot8, even, pltpu.roll(odd, 8, 1))
        ctot[1] = jnp.where(slot8, pltpu.roll(even, 120, 1), odd)
        for d in (3, 2, 4, 1, 5, 0, 6):
            ccp[d].start()

    to_right = [(z + d + 1) <= 7 for d in range(7)]
    ccp = [remote(ctot.at[jnp.where(to_right[d], 0, 1)], crcv.at[d], k_s.at[d], k_r.at[d], chips[d]) for d in range(7)]

    def local_y(l, carry):
        at = pl.multiple_of(l * BX, BX)
        tt = pl.multiple_of(l * BY, BY)
        mean = total[pl.ds(at, BX), :] * (1.0 / MEMBERS)
        gr = grad_v[pl.ds(at, BX), :]
        v = jnp.concatenate([(mem_v[k, pl.ds(at, BX), :].astype(F32) - mean) * gr for k in range(KLOC)], axis=0)
        n = KLOC * BX
        both = jnp.concatenate([thi[pl.ds(tt, BY), :], tlo[pl.ds(tt, BY), :]], axis=1)
        res = dot(jnp.concatenate(split(v), axis=0), both, NN)
        res = res[:n, :BY] + res[n:, :BY] + res[:n, BY:]
        zbuf[0, pl.ds(at, BX), :] = res[0:BX]
        zbuf[1, pl.ds(at, BX), :] = res[BX:]
        return carry

    def synth(g, carry):
        at = pl.multiple_of(g * 64, 64)
        k8 = kap[pl.ds(pl.multiple_of(g * 8, 8), 8), :]
        big = jnp.concatenate([jnp.where(lane8 == lv, k8, 0.0) for lv in range(4)], axis=0)
        kh, kl = split(big)
        wh, wl = split(wtab[pl.ds(pl.multiple_of(g * 32, 32), 32), :])
        res = dot(jnp.concatenate([kh, kl, kh], axis=0), jnp.concatenate([wh, wh, wl], axis=0), TN)
        zbuf[0, pl.ds(at, 64), :] += res[0:64]
        zbuf[1, pl.ds(at, 64), :] += res[64:]
        return carry

    def block():
        for cp in ag:
            cp.wait()
        lax.fori_loop(0, LEV, local_y, 0, unroll=8)
        lax.fori_loop(0, GROUPS, synth, 0, unroll=4)


    rounds(2)
    spread()
    for load in loads[3:5]:
        load.wait()
    alpha = lx.rate / (1.0 + a_sub)
    scale = 2.0 * lx.rate * lx.rate * lx.rate * alpha * alpha
    pid = iota((LEV, LEV), 0)
    lid = iota((LEV, LEV), 1)
    keep = jnp.abs(pid - lid) <= bands[...]
    mixed = jnp.where(keep, weights[...], 0.0) * scale[:, 0:LEV]
    mh, ml = split(mixed.T)
    mcat = jnp.concatenate([mh, mh, ml], axis=1)

    def rest():
        block()

    rest()
    collect()

    for k in range(KLOC):
        for q in range(4):
            row = (k * 4 + q) * LEV
            xr[row:row + LEV, :] = jnp.where(core == k, xlo[q // 2, q % 2], xsr[q // 2, q % 2])

    def local_x(l, carry):
        tt = pl.multiple_of(l * BY, BY)
        vh, vl = split(xr[pl.ds(l, 8, stride=LEV), :])
        th = thi[pl.ds(tt, BY), :]
        xf[pl.ds(l, 8, stride=LEV), :] = dot(jnp.concatenate([vh, vl, vh], axis=1),
                                             jnp.concatenate([th, th, tlo[pl.ds(tt, BY), :]], axis=0), NN)
        return carry

    lax.fori_loop(0, LEV, local_x, 0, unroll=16)
    for cp in ccp:
        cp.wait()
    to_me, to_us = jnp.zeros((8, 128), F32), jnp.zeros((8, 128), F32)
    for d in range(7):
        from_left = (z - (d + 1)) >= 0
        to_me = to_me + jnp.where(from_left, crcv[d], 0.0)
        to_us = to_us + jnp.where(from_left, 0.0, crcv[d])
    mate = jnp.where((slot < 8) == (core == 1), csib[...], 0.0)
    cown[...] = mate
    cown[pl.ds(0, 8, stride=2), :] += jnp.where(slot8, to_me, pltpu.roll(to_us, 8, 1))
    cown[pl.ds(1, 8, stride=2), :] += jnp.where(slot8, pltpu.roll(to_me, 120, 1), to_us)
    zr, zc = iota((64, 256), 0), iota((64, 256), 1)
    fits = ((zr // 32 == (zc // 64) % 2) & ((zr // 8) % 4 == (zc // 4) % 4)
            & ((zr % 8) // 4 == zc // 128) & (zr % 4 == (zc // 16) % 4))

    def synth_x(t, carry):
        row = jnp.concatenate([cown[pl.ds(2 * t, 1), :], cown[pl.ds(2 * t + 1, 1), :]], axis=1)
        kh, kl = split(jnp.where(fits, jnp.broadcast_to(row, (64, 256)), 0.0))
        w = wtab[pl.ds(pl.multiple_of(t * 64, 64), 64), :]
        tiles = [w[(g * 4 + lv) * 8:(g * 4 + lv) * 8 + 8] for g in range(2) for k in range(2)
                 for lv in range(4) for twice in range(2)]
        wh, wl = split(jnp.concatenate(tiles, axis=0))
        res = dot(kh, wh, NN) + dot(kl, wh, NN) + dot(kh, wl, NN)
        for j in range(8):
            xf[pl.ds(pl.multiple_of(j * LEV + t * 8, 8), 8), :] += res[j * 8:(j + 1) * 8]
        return carry

    lax.fori_loop(0, LEV // 8, synth_x, 0, unroll=8)

    g, s, e, G = lx.g, lx.s, lx.e, lx.G
    ge = 1.0 + g
    p_s, p_e, p_me, p_2e = lx.power(s), lx.power(e), lx.power(-e), lx.power(2.0 * NX - e)
    hx = p_e - p_2e
    ux = p_e * (e + G) - p_2e * (2.0 * NX - e + G)
    hs = p_s - lx.power(2.0 * NX - s)
    p_s1, p_1e = lx.power(s - 1.0), lx.power(1.0 - e)
    near_s, far_s = lx.reach(s)
    near_e, far_e = lx.reach(e)

    for k in range(KLOC):
        for t in range(LEV // 8):
            lo = t * 8
            cut = lambda m: m[lo:lo + 8]
            sa, sb, la, lh = [xf[(k * 4 + q) * LEV + lo:(k * 4 + q) * LEV + lo + 8, :] for q in range(4)]
            a8, ge8, hx8, pm8 = cut(a_sub), cut(ge), cut(hx), cut(p_me)
            line = [zbuf[k, pl.ds(lo * BX + x, 8, stride=BX), :] for x in range(BX)]

            def sweep(run, order):
                for x in range(BX)[::order]:
                    run = a8 * run + line[x]
                    line[x] = run
                return run

            sa_e = cut(p_1e) * sweep(cut(p_s1) * sa, 1)
            first = sweep(ge8 * (hx8 * sa_e + pm8 * lh), -1)
            lh_s = cut(p_s) * (first / ge8 - cut(hs) * sa)
            last = sweep(ge8 * (cut(p_s1) * (cut(near_s) * sa - sb) + cut(far_s) * lh_s), 1)
            sb_e = cut(near_e) * sa_e - cut(p_1e) * (last / ge8 - cut(far_e) * lh)
            sweep(ge8 * ge8 * (cut(ux) * sa_e - hx8 * sb_e + pm8 * la - (e * pm8 + cut(g) * cut(p_e)) * lh), -1)
            for x in range(BX):
                fbuf[k, x, lo:lo + 8, :] = line[x]

    def mix(x, carry):
        for k in range(KLOC):
            fh, fl = split(fbuf[k, x])
            fcat = jnp.concatenate([fh, fl, fh], axis=0)
            out[k, pl.ds(x, LEV, stride=BX), :] = dot(mcat, fcat, NN)
        return carry

    lax.fori_loop(0, BX, mix, 0, unroll=8)


def per_device(members, gradient, control, filter_rates, vertical_weights, band_widths):
    hbm = pl.BlockSpec(memory_space=pltpu.HBM)
    dma = pltpu.SemaphoreType.DMA

    def vm(*shape):
        return pltpu.VMEM(shape, F32)

    three = [dma((3,))] * 2
    single = [dma] * 2
    out = pl.pallas_call(
        kernel,
        out_shape=pltpu.VMEM((KLOC, ROWS, BY), F32),
        in_specs=[hbm] * 5,
        out_specs=pl.BlockSpec(memory_space=pltpu.VMEM),
        scratch_shapes=[
            pltpu.SMEM((LEV,), F32),
            pltpu.VMEM((1, LEV), jnp.int32),
            vm(LEV, LEV),
            pltpu.VMEM((KLOC, ROWS, BY), BF16),
            vm(ROWS, BY),
            vm(ROWS, BY), vm(ROWS, BY), vm(3, QUARTER, BY),
            vm(KLOC, ROWS, BY), vm(KLOC, ROWS, BY),
            vm(LEV * 8, 128), vm(LEV, 128),
            pltpu.VMEM((LEV * BY, BY), BF16),
            pltpu.VMEM((LEV * BY, BY), BF16),
            vm(GROUPS * 8, 128),
            vm(2, GROUPS, 128), vm(3, 2, GROUPS, 128),
            vm(4, LEV, 128), vm(4, LEV, 128), vm(4, LEV, 128), vm(4, LEV, 128),
            vm(4, GROUPS, 128), vm(3, 2, GROUPS, 128), vm(4, GROUPS, 128), vm(4, GROUPS, 128),
            vm(GROUPS * 8, 128),
            vm(KLOC, 4, LEV, 128), vm(4, LEV, 128),
            vm(3, 2, 2, LEV, 128), vm(3, 2, 2, LEV, 128), vm(2, 2, LEV, 128), vm(2, 2, LEV, 128), vm(2, 2, LEV, 128),
            vm(GROUPS, 128), vm(GROUPS, 128), vm(2, 8, 128), vm(7, 8, 128),
            vm(8 * LEV, 128), vm(8 * LEV, 128),
            vm(KLOC, BX, LEV, BY),
            dma((5,)),
            *three, *three, *three, dma((2, 2, PARTS)), dma((2, 2, PARTS)), *three,
            *single, dma((PARTS,)), dma((PARTS,)),
            dma((3, 2, PARTS)), dma((3, 2, PARTS)), dma((2,)), dma((2,)),
            dma((7,)), dma((7,)), *single,
        ],
        compiler_params=pltpu.CompilerParams(
            collective_id=0, has_side_effects=True, vmem_limit_bytes=48 << 20),
        name="localize",
    )(*[
        pltpu.with_memory_space_constraint(v, pltpu.HBM)
        for v in (filter_rates, band_widths.reshape(1, LEV), vertical_weights,
                  members.reshape(KLOC, ROWS, BY), gradient.reshape(ROWS, BY))
    ])
    return out.reshape(KLOC, LEV, BX, BY) + control.astype(F32)


def solution(mesh):
    placed = (
        P("mem", None, "gx", "gy"),
        P(None, "gx", "gy"),
        P("mem", None, "gx", "gy"),
        P(),
        P(),
        P(),
    )
    return jax.shard_map(
        per_device,
        mesh=mesh,
        in_specs=placed,
        out_specs=P("mem", None, "gx", "gy"),
        check_vma=False,
    )
```
